512 devices in a mesh: chol: 16 (over z_lo, core), walk: 32 (over y, x, z_hi).
Axes of the slice: x: 4, y: 4, z: 16 (z_hi: 2, z_lo: 8; z = z_hi * 8 + z_lo), core: 2. Of those that a mesh axis runs over, the one named last changes fastest.
Arguments:
- orbitals: float32 [32, 1024, 200], P('walk', 'chol'), may hold values from -6 to 6
- inverse_intersection: float32 [32, 200, 200], P('walk'), may hold values from -0.4375 to 0.4375
- half_rotated: bfloat16 [16, 200, 1024], P('chol'), may hold values from -0.013671875 to 0.013671875
- chol_full: bfloat16 [16, 1024, 1024], P('chol', 'walk'), as said below
- fields: float32 [16, 32], P('chol', 'walk'), may hold values from -6 to 6
Outputs:
- orbitals_next: float32 [32, 1024, 200], P('walk', 'chol')
The draws below stay inside these ranges and needn't reach their ends.
Inputs may be any that keep to these rules, and one draw needn't show every extreme that they name: Every 1024 x 1024 matrix chol_full[g] is symmetric.
All inputs are finite; a program needn't handle non-finite values.
Results may differ from the reference program's by a relative error of at most 0.0041.
Values may be sent and summed in bfloat16 or wider, within the bound.
No kernel may reach another device: no remote copies, remote signals or barrier semaphores. Data moves between devices by JAX's collectives and lax.ppermute only.
A program may use at most 64 MiB of HBM per device.

```python
import jax
import jax.numpy as jnp
from jax import lax

N = 1024
O = 200
TAYLOR = 5
G_DEV = 1
G = 16
W = 32


def draw_chol_full(key, part):
    key = jax.random.fold_in(key, 7)
    values = jax.random.uniform(key, (G, N, N), jnp.float32, -1.0, 1.0)
    scale = (1.5 / (N * G_DEV)) ** 0.5
    return ((values + jnp.swapaxes(values, 1, 2)) * scale).astype(jnp.bfloat16)


def block_scale(stream_key, shape, split, smallest, largest):
    def one(position, parts):
        steps = jax.random.uniform(jax.random.fold_in(jax.random.fold_in(stream_key, 6), position), (parts,), jnp.float32, smallest / len(split), largest / len(split))
        return jnp.repeat(jnp.exp(steps), shape[position] // parts).reshape((-1,) + (1,) * (len(shape) - position - 1))

    loudness = one(*split[0])
    for cut in split[1:]:
        loudness = loudness * one(*cut)
    return loudness


def noise(stream_key, extent, scale, most, pieces=(), dtype=jnp.bfloat16):
    drawn = scale * jax.random.normal(stream_key, extent, jnp.float32)
    if pieces:
        drawn = drawn * block_scale(stream_key, extent, pieces, -0.22, 0.18)
    return jnp.clip(drawn, -most, most).astype(dtype)


def setup_inputs(seed: int = 0) -> dict:
    key_list = jax.random.split(jax.random.key(seed), 6)
    orbitals = noise(key_list[0], (W, N, O), 1.0, 6.0, ((0, 32), (1, 16)), jnp.float32)
    inverse_intersection = noise(key_list[1], (W, O, O), O ** -0.5, 0.4375, ((0, 32),), jnp.float32)
    half_rotated = noise(key_list[2], (G, O, N), (N * O) ** -0.5, 0.013671875, ((0, 16),))
    chol_full = draw_chol_full(jax.random.fold_in(key_list[5], 71), 0)
    fields = noise(key_list[4], (G, W), 1.0, 6.0, ((0, 16), (1, 32)), jnp.float32)
    return {"orbitals": orbitals, "inverse_intersection": inverse_intersection, "half_rotated": half_rotated, "chol_full": chol_full, "fields": fields}


field_scale = 0.4


def reference(orbitals, inverse_intersection, half_rotated, chol_full, fields):
    highest = lax.Precision.HIGHEST
    theta_all = jnp.einsum('wno,wop->wnp', orbitals, inverse_intersection, precision=highest).astype(jnp.bfloat16)
    raw_bias = jnp.einsum('gon,wno->gw', half_rotated.astype(jnp.float32), theta_all.astype(jnp.float32), precision=highest)
    shifted = field_scale * (fields - jnp.clip(raw_bias, -1.0, 1.0))
    vectors = chol_full.astype(jnp.float32)

    def propagate(inputs):
        walker, weights = inputs
        operator = jnp.einsum('g,gmn->mn', weights, vectors, precision=highest)
        taylor_term = walker.astype(jnp.bfloat16)
        result = walker
        for degree in range(1, TAYLOR + 1):
            applied = jnp.dot(operator, taylor_term.astype(jnp.float32), precision=highest)
            result = result + applied / degree
            taylor_term = (applied / degree).astype(jnp.bfloat16)
        return result

    return lax.map(propagate, (orbitals, shifted.T))
```

```python
import jax
import jax.numpy as jnp
from jax import lax
from jax.experimental import pallas as pl
from jax.experimental.pallas import tpu as pltpu
from jax.sharding import Mesh, PartitionSpec as P

TAYLOR = 5
field_scale = 0.4
f32, bf16 = jnp.float32, jnp.bfloat16

CHOL = ("zl", "core")
WALK = ("y", "x", "zh")
PLANE = ("y", "x")
HIGHEST = lax.Precision.HIGHEST
NT = (((1,), (1,)), ((), ()))


def iota(shape, dim):
    return lax.broadcasted_iota(jnp.int32, shape, dim)


def plane_index():
    return lax.axis_index("y") * 4 + lax.axis_index("x")


def chol_index():
    return lax.axis_index("zl") * 2 + lax.axis_index("core")


def first_kernel(orb_ref, inv_ref, hr_ref, chol_ref, theta_ref, hrc_ref, piece_ref, low_ref, rows_lo, rows_hi):
    p = plane_index()
    start = p // 2
    for d in range(5):
        col = pl.multiple_of(lax.rem(start + d, 8) * 128, 128)
        piece_ref[:, 128 * d:128 * d + 128] = chol_ref[:, pl.ds(col, 128)]
    rows_lo[...] = jnp.zeros_like(rows_lo)
    rows_hi[...] = jnp.zeros_like(rows_hi)
    for i in range(13):
        @pl.when(p == i)
        def _():
            if i < 12:
                both = hr_ref[16 * i:16 * i + 16, :].astype(f32)
                rows_lo[...] = both[0:8]
                rows_hi[...] = both[8:16]
            else:
                rows_lo[...] = hr_ref[192:200, :].astype(f32)
    left = iota((8, 128), 1) < 64
    for u in range(8):
        low = rows_lo[:, 128 * u:128 * u + 128]
        high = rows_hi[:, 128 * u:128 * u + 128]
        hrc_ref[2 * u] = jnp.where(left, low, pltpu.roll(high, 64, 1)).astype(bf16)
        hrc_ref[2 * u + 1] = jnp.where(left, pltpu.roll(low, 64, 1), high).astype(bf16)
    orb = orb_ref[...]
    twice = jnp.concatenate([orb, orb], axis=0)
    theta_t = lax.dot_general(inv_ref[...], twice, (((0,), (1,)), ((), ())), precision=HIGHEST,
                              preferred_element_type=f32)
    for i in range(16):
        if i < 12:
            tile = jnp.where(left, theta_t[16 * i:16 * i + 8], theta_t[16 * i + 8:16 * i + 16])
        elif i == 12:
            tile = jnp.where(left, theta_t[192:200], 0.0)
        else:
            tile = jnp.zeros((8, 128), f32)
        theta_ref[i] = tile.astype(bf16)
    low_ref[...] = jnp.concatenate([orb, jnp.zeros((64, 56), f32)], axis=1).astype(bf16)


def bias_kernel(field_ref, hr_ref, theta_ref, out_ref):
    p = plane_index()
    h = hr_ref[...].astype(f32).reshape(128, 128).astype(bf16)
    t = theta_ref[...].astype(f32).reshape(128, 128).astype(bf16)
    pairs = lax.dot_general(h, t, NT, preferred_element_type=f32)
    row, col = iota((128, 128), 0), iota((128, 128), 1)
    pairs = jnp.where((row & 7) == (col & 7), pairs, 0.0)
    by_vector = pairs.reshape(16, 8, 128).sum(axis=1)
    gather = jnp.where((row >> 3) == col, 1.0, 0.0).astype(f32)
    part = jnp.dot(by_vector, gather, precision=HIGHEST, preferred_element_type=f32)
    tile = part + jnp.where(iota((16, 128), 1) == 16 + p, field_ref[0, 0], 0.0)
    for j in range(16):
        out_ref[j] = tile


def plane_sum_kernel(in_ref, out_ref):
    total = jnp.sum(in_ref[...], axis=0)
    row, col = iota((16, 128), 0), iota((16, 128), 1)
    tile = jnp.where((col < 16) | (row == chol_index()), total, 0.0)
    for j in range(16):
        out_ref[j] = tile


def operator_kernel(in_ref, near_ref, far_ref, out_ref):
    base = lax.axis_index("zl") * 2 + lax.axis_index("zh")
    total = jnp.sum(in_ref[...], axis=0)
    fields = pltpu.roll(total, 112, 1)
    shifted = field_scale * (fields - jnp.clip(total, -1.0, 1.0))
    shifted = jnp.where(iota((16, 128), 1) < 16, shifted, 0.0)
    by_walker = jnp.concatenate([shifted, jnp.zeros((112, 128), f32)], axis=0).T
    high = by_walker.astype(bf16)
    rest = (by_walker - high.astype(f32)).astype(bf16)
    g, q = iota((128, 512), 0), iota((128, 512), 1) >> 5
    j = q >> 1
    code = ((j & 1) << 3) | ((j & 2) << 1) | ((j & 4) >> 1) | (q & 1)
    pick = jnp.where(g == (code ^ base), 1.0, 0.0).astype(bf16)
    walkers = jnp.where((iota((512, 128), 0) >> 5) == iota((512, 128), 1), 1.0, 0.0).astype(bf16)
    same = (iota((512, 512), 0) & 31) == (iota((512, 512), 1) & 31)

    def weights(part):
        spread = jnp.dot(part, pick, preferred_element_type=f32).astype(bf16)
        full = jnp.dot(walkers, spread, preferred_element_type=f32)
        return jnp.where(same, full, 0.0).astype(bf16)

    w_high, w_rest = weights(high), weights(rest)
    near, far = near_ref[:, 0:640], far_ref[:, 0:640]
    for i in range(2):
        rows = slice(256 * i, 256 * i + 256)
        value = jnp.dot(w_rest[rows, :256], near, preferred_element_type=f32)
        value += jnp.dot(w_rest[rows, 256:], far, preferred_element_type=f32)
        value += jnp.dot(w_high[rows, :256], near, preferred_element_type=f32)
        value += jnp.dot(w_high[rows, 256:], far, preferred_element_type=f32)
        out_ref[rows, :] = value.astype(bf16)


def taylor_kernel(orb_ref, mine_ref, other_ref, low_mine_ref, low_other_ref, out_ref, op, term_a, term_b):
    z, k = lax.axis_index("zl"), lax.axis_index("core")
    order = (0, 4, 2, 6, 1, 5, 3, 7)
    for j in range(8):
        block = 2 * (z ^ order[j])
        here = pl.multiple_of((block + k) * 64, 64)
        there = pl.multiple_of((block + 1 - k) * 64, 64)
        term_a[pl.ds(here, 64), :] = low_mine_ref[64 * j:64 * j + 64, :]
        term_a[pl.ds(there, 64), :] = low_other_ref[64 * j:64 * j + 64, :]
    for p in range(16):
        here = pl.multiple_of(64 * p + 32 * k, 32)
        there = pl.multiple_of(64 * p + 32 * (1 - k), 32)
        for d in range(5):
            col = ((p // 2 + d) % 8) * 128
            op[pl.ds(here, 32), col:col + 128] = mine_ref[p, :, 128 * d:128 * d + 128]
            op[pl.ds(there, 32), col:col + 128] = other_ref[p, :, 128 * d:128 * d + 128]
    for i in range(8):
        for d in range(1, 4):
            j = (i + d) % 8
            block = op[128 * i:128 * i + 128, 128 * j:128 * j + 128].astype(f32)
            op[128 * j:128 * j + 128, 128 * i:128 * i + 128] = block.T.astype(bf16)
    own = pl.multiple_of((2 * z + k) * 64, 64)
    own_rows = op[pl.ds(own, 64), :]
    total = jnp.zeros((64, 256), f32)
    now, later = term_a, term_b
    for degree in range(1, TAYLOR + 1):
        term = now[...]
        total += jnp.dot(own_rows, term, preferred_element_type=f32) * (1.0 / degree)
        if degree < TAYLOR:
            for i in range(4):
                image = jnp.dot(op[256 * i:256 * i + 256, :], term, preferred_element_type=f32)
                later[256 * i:256 * i + 256, :] = (image * (1.0 / degree)).astype(bf16)
            now, later = later, now
    out_ref[...] = orb_ref[...] + total[:, :200]


def call(body, outs, *args, scratch=(), smem=0):
    vmem = pl.BlockSpec(memory_space=pltpu.VMEM)
    specs = [pl.BlockSpec(memory_space=pltpu.SMEM)] * smem + [vmem] * (len(args) - smem)
    many = isinstance(outs, (list, tuple))
    return pl.pallas_call(
        body,
        out_shape=outs,
        in_specs=specs,
        out_specs=[vmem] * len(outs) if many else vmem,
        scratch_shapes=list(scratch),
        compiler_params=pltpu.CompilerParams(vmem_limit_bytes=40 * 2**20),
    )(*args)


def shape(dims, dtype):
    return jax.ShapeDtypeStruct(dims, dtype)


def exchange(value, axes):
    return lax.all_to_all(value, axes, 0, 0, tiled=True)


def shards(orbitals, inverse_intersection, half_rotated, chol_full, fields):
    orb = orbitals[0]
    theta, hr_cut, piece, low = call(
        first_kernel,
        [shape((16, 8, 128), bf16), shape((16, 8, 128), bf16), shape((32, 640), bf16), shape((64, 256), bf16)],
        orb, inverse_intersection[0], half_rotated[0], chol_full[0],
        scratch=[pltpu.VMEM((8, 1024), f32), pltpu.VMEM((8, 1024), f32)],
    )
    pairs = [(k * 2 + h, h * 2 + k) for k in range(2) for h in range(2)]
    cross = [(k * 2 + h, h * 2 + 1 - k) for k in range(2) for h in range(2)]
    straight = lax.ppermute(piece, ("core", "zh"), pairs)
    crossed = lax.ppermute(piece, ("core", "zh"), cross)
    hr_all = exchange(hr_cut, CHOL)
    held = jnp.concatenate([jnp.concatenate([straight, crossed], axis=0), low], axis=1)

    def swap(value, bit):
        return lax.ppermute(value, "zl", [(i, i ^ bit) for i in range(8)])

    theta_all = exchange(theta, PLANE)
    held = jnp.concatenate([held, swap(held, 4)], axis=0)
    partial = call(bias_kernel, shape((16, 16, 128), f32), fields, hr_all, theta_all, smem=1)
    in_plane = exchange(partial, PLANE)
    held = jnp.concatenate([held, swap(held, 2)], axis=0)
    summed = call(plane_sum_kernel, shape((16, 16, 128), f32), in_plane)
    everywhere = exchange(summed, CHOL)
    far = swap(held, 1)
    lows = jnp.concatenate([held[:, 640:], far[:, 640:]], axis=0)
    swap_core = [(0, 1), (1, 0)]
    lows_other = lax.ppermute(lows, "core", swap_core)
    pieces = call(operator_kernel, shape((512, 640), bf16), everywhere, held, far)
    mine = exchange(pieces.reshape(16, 32, 640), PLANE)
    other = lax.ppermute(mine, "core", swap_core)
    out = call(
        taylor_kernel, shape((64, 200), f32), orb, mine, other, lows, lows_other,
        scratch=[pltpu.VMEM((1024, 1024), bf16), pltpu.VMEM((1024, 256), bf16), pltpu.VMEM((1024, 256), bf16)],
    )
    return out[None]


def solution(mesh):
    fine = Mesh(mesh.devices.reshape(8, 2, 4, 4, 2), ("zl", "core", "y", "x", "zh"))
    return jax.shard_map(
        shards,
        mesh=fine,
        in_specs=(
            P(WALK, CHOL, None),
            P(WALK, None, None),
            P(CHOL, None, None),
            P(CHOL, WALK, None),
            P(CHOL, WALK),
        ),
        out_specs=P(WALK, CHOL, None),
        check_vma=False,
    )
```

```python
import jax
import jax.numpy as jnp
from jax import lax
from jax.experimental import pallas as pl
from jax.experimental.pallas import tpu as pltpu
from jax.sharding import Mesh, PartitionSpec as P

TAYLOR = 5
field_scale = 0.4
f32, bf16 = jnp.float32, jnp.bfloat16

CHOL = ("zl", "core")
WALK = ("y", "x", "zh")
PLANE = ("y", "x")
HIGHEST = lax.Precision.HIGHEST
NT = (((1,), (1,)), ((), ()))


def iota(shape, dim):
    return lax.broadcasted_iota(jnp.int32, shape, dim)


def plane_index():
    return lax.axis_index("y") * 4 + lax.axis_index("x")


def chol_index():
    return lax.axis_index("zl") * 2 + lax.axis_index("core")


def first_kernel(field_ref, orb_hbm, inv_hbm, hr_hbm, chol_hbm, theta_ref, hrc_ref, piece_ref,
                 orb_ref, inv_ref, hr_ref, chol_ref, rows_lo, rows_hi, sems):
    pairs = ((chol_hbm, chol_ref), (hr_hbm, hr_ref), (orb_hbm, orb_ref), (inv_hbm, inv_ref))
    copies = [pltpu.make_async_copy(src, dst, sems.at[i]) for i, (src, dst) in enumerate(pairs)]
    for copy in copies:
        copy.start()
    p = plane_index()
    copies[0].wait()
    start = p // 2
    for d in range(5):
        col = pl.multiple_of(lax.rem(start + d, 8) * 128, 128)
        piece_ref[:, 128 * d:128 * d + 128] = chol_ref[:, pl.ds(col, 128)]
    rows_lo[...] = jnp.zeros_like(rows_lo)
    rows_hi[...] = jnp.zeros_like(rows_hi)
    copies[1].wait()
    for i in range(13):
        @pl.when(p == i)
        def _():
            if i < 12:
                both = hr_ref[16 * i:16 * i + 16, :].astype(f32)
                rows_lo[...] = both[0:8]
                rows_hi[...] = both[8:16]
            else:
                rows_lo[...] = hr_ref[192:200, :].astype(f32)
    left = iota((8, 128), 1) < 64
    for u in range(8):
        low = rows_lo[:, 128 * u:128 * u + 128]
        high = rows_hi[:, 128 * u:128 * u + 128]
        hrc_ref[2 * u] = jnp.where(left, low, pltpu.roll(high, 64, 1)).astype(bf16)
        hrc_ref[2 * u + 1] = jnp.where(left, pltpu.roll(low, 64, 1), high).astype(bf16)
    copies[2].wait()
    copies[3].wait()
    orb = orb_ref[...]
    twice = jnp.concatenate([orb, orb], axis=0)
    theta_t = lax.dot_general(inv_ref[...], twice, (((0,), (1,)), ((), ())), precision=HIGHEST,
                              preferred_element_type=f32)
    for i in range(13):
        if i < 12:
            tile = jnp.where(left, theta_t[16 * i:16 * i + 8], theta_t[16 * i + 8:16 * i + 16])
        else:
            tile = jnp.where(left, theta_t[192:200], 0.0)
        theta_ref[i] = tile.astype(bf16)
    field = jnp.full((8, 128), field_ref[0, 0], f32)
    high = field.astype(bf16).astype(f32)
    middle = (field - high).astype(bf16).astype(f32)
    row = iota((8, 128), 0)
    parts = jnp.where(row == 0, high, jnp.where(row == 1, middle, jnp.where(row == 2, field - high - middle, 0.0)))
    theta_ref[13] = parts.astype(bf16)


def spread_kernel(hr_ref, theta_ref, out_ref):
    for j in range(16):
        out_ref[j, 0:16] = hr_ref[...]
        out_ref[j, 16:30] = theta_ref[...]


def bias_kernel(in_ref, out_ref):
    pairs = jnp.zeros((128, 128), f32)
    for i in range(13):
        h = in_ref[i, 0:16].astype(f32).reshape(128, 128).astype(bf16)
        t = in_ref[:, 16 + i].astype(f32).reshape(128, 128).astype(bf16)
        pairs += lax.dot_general(h, t, NT, preferred_element_type=f32)
    row, col = iota((128, 128), 0), iota((128, 128), 1)
    pairs = jnp.where((row & 7) == (col & 7), pairs, 0.0)
    by_vector = pairs.reshape(16, 8, 128).sum(axis=1)
    gather = jnp.where((row >> 3) == col, 1.0, 0.0).astype(f32)
    part = jnp.dot(by_vector, gather, precision=HIGHEST, preferred_element_type=f32)
    fields = in_ref[:, 29].astype(f32).sum(axis=1)
    row, col = iota((16, 128), 0), iota((16, 128), 1)
    fields = jnp.sum(jnp.where(col == row + 16, fields, 0.0), axis=0, keepdims=True)
    tile = part + jnp.where(row == chol_index(), fields, 0.0)
    for j in range(16):
        out_ref[j] = tile


def operator_kernel(in_ref, held_ref, one_ref, two_ref, three_ref, out_ref):
    base = lax.axis_index("zl") * 2 + lax.axis_index("zh")
    total = jnp.sum(in_ref[...], axis=0)
    fields = pltpu.roll(total, 112, 1)
    shifted = field_scale * (fields - jnp.clip(total, -1.0, 1.0))
    shifted = jnp.where(iota((16, 128), 1) < 16, shifted, 0.0)
    by_walker = jnp.concatenate([shifted, jnp.zeros((112, 128), f32)], axis=0).T
    high = by_walker.astype(bf16)
    rest = (by_walker - high.astype(f32)).astype(bf16)
    g, q = iota((128, 512), 0), iota((128, 512), 1) >> 5
    code = ((q & 2) << 2) | ((q & 12) >> 1) | (q & 1)
    pick = jnp.where(g == (code ^ base), 1.0, 0.0).astype(bf16)
    walkers = jnp.where((iota((512, 128), 0) >> 5) == iota((512, 128), 1), 1.0, 0.0).astype(bf16)
    same = (iota((512, 512), 0) & 31) == (iota((512, 512), 1) & 31)

    def weights(part):
        spread = jnp.dot(part, pick, preferred_element_type=f32).astype(bf16)
        full = jnp.dot(walkers, spread, preferred_element_type=f32)
        return jnp.where(same, full, 0.0).astype(bf16)

    w_high, w_rest = weights(high), weights(rest)
    vectors = jnp.concatenate([held_ref[...], one_ref[...], two_ref[...], three_ref[...]], axis=0)
    for i in range(2):
        rows = slice(256 * i, 256 * i + 256)
        value = jnp.dot(w_rest[rows], vectors, preferred_element_type=f32)
        value += jnp.dot(w_high[rows], vectors, preferred_element_type=f32)
        out_ref[rows, :] = value.astype(bf16)


def taylor_kernel(orb_ref, mine_ref, other_ref, all_hbm, out_ref, op, term_a, term_b, all_ref, sem):
    z, k = lax.axis_index("zl"), lax.axis_index("core")
    gathered = pltpu.make_async_copy(all_hbm, all_ref, sem)
    gathered.start()
    for p in range(16):
        here = pl.multiple_of(64 * p + 32 * k, 32)
        there = pl.multiple_of(64 * p + 32 * (1 - k), 32)
        for d in range(5):
            col = ((p // 2 + d) % 8) * 128
            op[pl.ds(here, 32), col:col + 128] = mine_ref[p, :, 128 * d:128 * d + 128]
            op[pl.ds(there, 32), col:col + 128] = other_ref[p, :, 128 * d:128 * d + 128]
    for i in range(8):
        for d in range(1, 4):
            j = (i + d) % 8
            block = op[128 * i:128 * i + 128, 128 * j:128 * j + 128].astype(f32)
            op[128 * j:128 * j + 128, 128 * i:128 * i + 128] = block.T.astype(bf16)
    gathered.wait()
    term_a[...] = jnp.concatenate([all_ref[...], jnp.zeros((1024, 56), f32)], axis=1).astype(bf16)
    own = pl.multiple_of((2 * z + k) * 64, 64)
    own_rows = op[pl.ds(own, 64), :]
    total = jnp.zeros((64, 256), f32)
    now, later = term_a, term_b
    for degree in range(1, TAYLOR + 1):
        term = now[...]
        total += jnp.dot(own_rows, term, preferred_element_type=f32) * (1.0 / degree)
        if degree < TAYLOR:
            for i in range(4):
                image = jnp.dot(op[256 * i:256 * i + 256, :], term, preferred_element_type=f32)
                later[256 * i:256 * i + 256, :] = (image * (1.0 / degree)).astype(bf16)
            now, later = later, now
    out_ref[...] = orb_ref[...] + total[:, :200]


def call(body, outs, *args, scratch=(), smem=0, hbm=(), grant=40):
    vmem = pl.BlockSpec(memory_space=pltpu.VMEM)
    specs = [pl.BlockSpec(memory_space=pltpu.SMEM)] * smem + [vmem] * (len(args) - smem)
    for i in hbm:
        specs[i] = pl.BlockSpec(memory_space=pl.ANY)
    many = isinstance(outs, (list, tuple))
    return pl.pallas_call(
        body,
        out_shape=outs,
        in_specs=specs,
        out_specs=[vmem] * len(outs) if many else vmem,
        scratch_shapes=list(scratch),
        compiler_params=pltpu.CompilerParams(vmem_limit_bytes=grant * 2**20),
    )(*args)


def shape(dims, dtype):
    return jax.ShapeDtypeStruct(dims, dtype)


def exchange(value, axes):
    return lax.all_to_all(value, axes, 0, 0, tiled=True)


def swap(value, bits):
    return lax.ppermute(value, "zl", [(i, i ^ bits) for i in range(8)])


def shards(orbitals, inverse_intersection, half_rotated, chol_full, fields):
    orb = orbitals[0]
    theta, hr_cut, piece = call(
        first_kernel,
        [shape((14, 8, 128), bf16), shape((16, 8, 128), bf16), shape((32, 640), bf16)],
        fields, orb, inverse_intersection[0], half_rotated[0], chol_full[0],
        scratch=[pltpu.VMEM((64, 200), f32), pltpu.VMEM((200, 200), f32), pltpu.VMEM((200, 1024), bf16),
                 pltpu.VMEM((32, 1024), bf16), pltpu.VMEM((8, 1024), f32), pltpu.VMEM((8, 1024), f32),
                 pltpu.SemaphoreType.DMA((4,))],
        smem=1, hbm=(1, 2, 3, 4), grant=60,
    )
    everyone = lax.all_gather(orb, CHOL, axis=0, tiled=True)
    pairs = [(k * 2 + h, h * 2 + k) for k in range(2) for h in range(2)]
    cross = [(k * 2 + h, h * 2 + 1 - k) for k in range(2) for h in range(2)]
    straight = lax.ppermute(piece, ("core", "zh"), pairs)
    crossed = lax.ppermute(piece, ("core", "zh"), cross)
    hr_all = exchange(hr_cut, CHOL)
    straight, crossed, hr_all = lax.optimization_barrier((straight, crossed, hr_all))
    held = jnp.concatenate([straight, crossed], axis=0)
    four = swap(held, 4)
    spread = call(spread_kernel, shape((16, 30, 8, 128), bf16), hr_all, theta)
    in_plane = exchange(spread, PLANE)
    four, in_plane = lax.optimization_barrier((four, in_plane))
    held = jnp.concatenate([held, four], axis=0)
    one, two, three = swap(held, 1), swap(held, 2), swap(held, 3)
    partial = call(bias_kernel, shape((16, 16, 128), f32), in_plane)
    everywhere = exchange(partial, CHOL)
    pieces = call(operator_kernel, shape((512, 640), bf16), everywhere, held, one, two, three)
    mine = exchange(pieces.reshape(16, 32, 640), PLANE)
    other = lax.ppermute(mine, "core", [(0, 1), (1, 0)])
    out = call(
        taylor_kernel, shape((64, 200), f32), orb, mine, other, everyone,
        scratch=[pltpu.VMEM((1024, 1024), bf16), pltpu.VMEM((1024, 256), bf16), pltpu.VMEM((1024, 256), bf16),
                 pltpu.VMEM((1024, 200), f32), pltpu.SemaphoreType.DMA(())],
        hbm=(3,), grant=60,
    )
    return out[None]


def solution(mesh):
    fine = Mesh(mesh.devices.reshape(8, 2, 4, 4, 2), ("zl", "core", "y", "x", "zh"))
    return jax.shard_map(
        shards,
        mesh=fine,
        in_specs=(
            P(WALK, CHOL, None),
            P(WALK, None, None),
            P(CHOL, None, None),
            P(CHOL, WALK, None),
            P(CHOL, WALK),
        ),
        out_specs=P(WALK, CHOL, None),
        check_vma=False,
    )
```

```python
import jax
import jax.numpy as jnp
from jax import lax
from jax.experimental import pallas as pl
from jax.experimental.pallas import tpu as pltpu
from jax.sharding import Mesh, PartitionSpec as P

TAYLOR = 5
field_scale = 0.4
f32, bf16 = jnp.float32, jnp.bfloat16

CHOL = ("zl", "core")
WALK = ("y", "x", "zh")
PLANE = ("y", "x")
RING = ("zh", "zl")


def iota(shape, dim):
    return lax.broadcasted_iota(jnp.int32, shape, dim)


def plane_index():
    return lax.axis_index("y") * 4 + lax.axis_index("x")


def chol_index():
    return lax.axis_index("zl") * 2 + lax.axis_index("core")


def pack_kernel(orb_hbm, chol_hbm, out_ref, orb_ref, chol_ref, sems):
    copies = [pltpu.make_async_copy(chol_hbm, chol_ref, sems.at[0]), pltpu.make_async_copy(orb_hbm, orb_ref, sems.at[1])]
    for copy in copies:
        copy.start()
    p = plane_index()
    start = p // 2

    def block(d):
        col = pl.multiple_of(lax.rem(start + d, 8) * 128, 128)
        return chol_ref[:, pl.ds(col, 128)]

    copies[0].wait()
    for d in range(4):
        out_ref[:, 128 * d:128 * d + 128] = block(d)
    last = block(4).astype(f32)
    half = jnp.bitwise_xor(jnp.bitwise_and(p, 1), (start >= 4).astype(jnp.int32))
    last = jnp.where(half == 1, pltpu.roll(last, 64, 1), last)
    copies[1].wait()
    low = jnp.concatenate([orb_ref[...], jnp.zeros((64, 56), f32)], axis=1)
    top, bottom = low[0:32], low[32:64]
    lane = iota((32, 128), 1)
    out_ref[:, 512:640] = jnp.where(lane < 64, last, pltpu.roll(bottom[:, 128:256], 64, 1)).astype(bf16)
    out_ref[:, 640:768] = top[:, 0:128].astype(bf16)
    out_ref[:, 768:896] = bottom[:, 0:128].astype(bf16)
    ends = jnp.where(lane < 72, top[:, 128:256], pltpu.roll(bottom[:, 128:256], 8, 1))
    out_ref[:, 896:976] = ends[:, 0:80].astype(bf16)


def select_kernel(ring_ref, own_ref, send_ref):
    k, h = lax.axis_index("core"), lax.axis_index("zh")
    lane = iota((32, 128), 1)
    for j in range(8):
        for half, target in ((k, own_ref), (1 - k, send_ref)):
            target[j, :, 0:512] = ring_ref[half, j, :, 0:512]
            tail = ring_ref[half, j, :, 512:640].astype(f32)
            target[j, :, 512:640] = jnp.where(lane < 64, tail, 0.0).astype(bf16)
        middle = ring_ref[h, j, :, 512:640].astype(f32)
        ends = jnp.concatenate([ring_ref[h, j, :, 896:976].astype(f32), jnp.zeros((32, 48), f32)], axis=1)
        top = jnp.where(lane < 72, ends, 0.0).astype(bf16)
        bottom = jnp.where(lane < 64, pltpu.roll(middle, 64, 1), jnp.where(lane < 72, pltpu.roll(ends, 120, 1), 0.0))
        bottom = bottom.astype(bf16)
        for target in (own_ref, send_ref):
            target[j, :, 640:768] = ring_ref[h, j, :, 640:768]
            target[j, :, 768:896] = top
            target[j, :, 896:1024] = ring_ref[h, j, :, 768:896]
            target[j, :, 1024:1152] = bottom


def bias_kernel(field_ref, own_ref, got_ref, inv_ref, hr_ref, term_ref, out_ref, inv_low, inv_high):
    k = lax.axis_index("core")
    for j in range(8):
        for source, core in ((own_ref, k), (got_ref, 1 - k)):
            row = pl.multiple_of((2 * j + core) * 64, 64)
            term_ref[pl.ds(row, 32), :] = source[j, :, 640:896]
            term_ref[pl.ds(row + 32, 32), :] = source[j, :, 896:1152]
    inverse = inv_ref[...]
    wide = jnp.concatenate([inverse, jnp.zeros((200, 56), f32)], axis=1)
    full = jnp.concatenate([wide, jnp.zeros((56, 256), f32)], axis=0)
    high = full.astype(bf16)
    inv_high[...] = high
    inv_low[...] = (full - high.astype(f32)).astype(bf16)
    term = term_ref[...]
    theta = jnp.dot(term, inv_high[...], preferred_element_type=f32)
    theta += jnp.dot(term, inv_low[...], preferred_element_type=f32)
    theta_high = theta.astype(bf16)
    theta_low = (theta - theta_high.astype(f32)).astype(bf16)
    rotated = hr_ref[...]
    product = jnp.dot(rotated, theta_high, preferred_element_type=f32)
    product += jnp.dot(rotated, theta_low, preferred_element_type=f32)
    diagonal = jnp.where(iota((200, 256), 0) == iota((200, 256), 1), product, 0.0)
    raw_bias = jnp.sum(jnp.sum(diagonal, axis=0, keepdims=True), axis=1, keepdims=True)
    shifted = field_scale * (field_ref[0, 0] - jnp.clip(raw_bias, -1.0, 1.0))
    here = (iota((16, 128), 0) == chol_index()) & (iota((16, 128), 1) == plane_index())
    tile = jnp.where(here, shifted, 0.0)
    for j in range(16):
        out_ref[j] = tile


def sum_kernel(in_ref, out_ref):
    tile = jnp.sum(in_ref[...], axis=0)
    for j in range(16):
        out_ref[j] = tile


def operator_kernel(in_ref, own_ref, got_ref, out_ref):
    k = lax.axis_index("core")
    shifted = jnp.sum(in_ref[...], axis=0)
    by_walker = jnp.concatenate([shifted, jnp.zeros((112, 128), f32)], axis=0).T
    high = by_walker.astype(bf16)
    rest = (by_walker - high.astype(f32)).astype(bf16)
    g, q = iota((128, 512), 0), iota((128, 512), 1) >> 5
    vector = 2 * (q & 7) + jnp.where(q < 8, k, 1 - k)
    pick = jnp.where(g == vector, 1.0, 0.0).astype(bf16)
    walkers = jnp.where((iota((512, 128), 0) >> 5) == iota((512, 128), 1), 1.0, 0.0).astype(bf16)
    same = (iota((512, 512), 0) & 31) == (iota((512, 512), 1) & 31)

    def weights(part):
        spread = jnp.dot(part, pick, preferred_element_type=f32).astype(bf16)
        full = jnp.dot(walkers, spread, preferred_element_type=f32)
        return jnp.where(same, full, 0.0).astype(bf16)

    w_high, w_rest = weights(high), weights(rest)
    own = own_ref[:, :, 0:640].reshape(256, 640)
    got = got_ref[:, :, 0:640].reshape(256, 640)
    vectors = jnp.concatenate([own, got], axis=0)
    for i in range(2):
        rows = slice(256 * i, 256 * i + 256)
        value = jnp.dot(w_rest[rows], vectors, preferred_element_type=f32)
        value += jnp.dot(w_high[rows], vectors, preferred_element_type=f32)
        out_ref[rows, :] = value.astype(bf16)


def taylor_kernel(orb_ref, mine_ref, other_ref, first_ref, out_ref, op, tail, term_a, term_b):
    k = lax.axis_index("core")
    for p in range(16):
        here = pl.multiple_of(64 * p + 32 * k, 32)
        there = pl.multiple_of(64 * p + 32 * (1 - k), 32)
        for row, source in ((here, mine_ref), (there, other_ref)):
            for d in range(4):
                col = ((p // 2 + d) % 8) * 128
                op[pl.ds(row, 32), col:col + 128] = source[p, :, 128 * d:128 * d + 128]
            tail[pl.ds(row, 32), :] = source[p, :, 512:640].astype(f32)
    for i in range(8):
        for d in range(1, 4):
            j = (i + d) % 8
            block = op[128 * i:128 * i + 128, 128 * j:128 * j + 128].astype(f32)
            op[128 * j:128 * j + 128, 128 * i:128 * i + 128] = block.T.astype(bf16)
    left = iota((64, 128), 1) < 64
    for i in range(4):
        j = i + 4
        near = tail[128 * i:128 * i + 128, :]
        far = tail[128 * j:128 * j + 128, :].T[0:64]
        top = jnp.where(left, near[0:64], far)
        bottom = jnp.where(left, far, pltpu.roll(near[64:128], 64, 1))
        block = jnp.concatenate([top, bottom], axis=0)
        op[128 * i:128 * i + 128, 128 * j:128 * j + 128] = block.astype(bf16)
        op[128 * j:128 * j + 128, 128 * i:128 * i + 128] = block.T.astype(bf16)
    own = pl.multiple_of(chol_index() * 64, 64)
    own_rows = op[pl.ds(own, 64), :]
    total = jnp.zeros((64, 256), f32)
    now, later, spare = first_ref, term_a, term_b
    for degree in range(1, TAYLOR + 1):
        term = now[...]
        total += jnp.dot(own_rows, term, preferred_element_type=f32) * (1.0 / degree)
        if degree < TAYLOR:
            for i in range(4):
                image = jnp.dot(op[256 * i:256 * i + 256, :], term, preferred_element_type=f32)
                later[256 * i:256 * i + 256, :] = (image * (1.0 / degree)).astype(bf16)
            now, later, spare = later, spare, later
    out_ref[...] = orb_ref[...] + total[:, :200]


def call(body, outs, *args, scratch=(), smem=0, hbm=(), grant=40):
    vmem = pl.BlockSpec(memory_space=pltpu.VMEM)
    specs = [pl.BlockSpec(memory_space=pltpu.SMEM)] * smem + [vmem] * (len(args) - smem)
    for i in hbm:
        specs[i] = pl.BlockSpec(memory_space=pl.ANY)
    many = isinstance(outs, (list, tuple))
    return pl.pallas_call(
        body,
        out_shape=outs,
        in_specs=specs,
        out_specs=[vmem] * len(outs) if many else vmem,
        scratch_shapes=list(scratch),
        compiler_params=pltpu.CompilerParams(vmem_limit_bytes=grant * 2**20),
    )(*args)


def shape(dims, dtype):
    return jax.ShapeDtypeStruct(dims, dtype)


def exchange(value, axes):
    return lax.all_to_all(value, axes, 0, 0, tiled=True)


def shards(orbitals, inverse_intersection, half_rotated, chol_full, fields):
    orb = orbitals[0]
    packed = call(
        pack_kernel, shape((32, 976), bf16), orb, chol_full[0],
        scratch=[pltpu.VMEM((64, 200), f32), pltpu.VMEM((32, 1024), bf16), pltpu.SemaphoreType.DMA((2,))],
        hbm=(0, 1), grant=60,
    )
    ring = lax.all_gather(packed, RING, axis=0, tiled=True)
    own, send = call(select_kernel, [shape((8, 32, 1152), bf16)] * 2, ring.reshape(2, 8, 32, 976))
    swap_core = [(0, 1), (1, 0)]
    got = lax.ppermute(send, "core", swap_core)
    first, partial = call(
        bias_kernel, [shape((1024, 256), bf16), shape((16, 16, 128), f32)],
        fields, own, got, inverse_intersection[0], half_rotated[0],
        scratch=[pltpu.VMEM((256, 256), bf16), pltpu.VMEM((256, 256), bf16)], smem=1,
    )
    in_plane = exchange(partial, PLANE)
    summed = call(sum_kernel, shape((16, 16, 128), f32), in_plane)
    everywhere = exchange(summed, CHOL)
    pieces = call(operator_kernel, shape((512, 640), bf16), everywhere, own, got)
    mine = exchange(pieces.reshape(16, 32, 640), PLANE)
    other = lax.ppermute(mine, "core", swap_core)
    out = call(
        taylor_kernel, shape((64, 200), f32), orb, mine, other, first,
        scratch=[pltpu.VMEM((1024, 1024), bf16), pltpu.VMEM((1024, 128), f32),
                 pltpu.VMEM((1024, 256), bf16), pltpu.VMEM((1024, 256), bf16)],
    )
    return out[None]


def solution(mesh):
    fine = Mesh(mesh.devices.reshape(8, 2, 4, 4, 2), ("zl", "core", "y", "x", "zh"))
    return jax.shard_map(
        shards,
        mesh=fine,
        in_specs=(
            P(WALK, CHOL, None),
            P(WALK, None, None),
            P(CHOL, None, None),
            P(CHOL, WALK, None),
            P(CHOL, WALK),
        ),
        out_specs=P(WALK, CHOL, None),
        check_vma=False,
    )
```

```python
import jax
import jax.numpy as jnp
from jax import lax
from jax.experimental import pallas as pl
from jax.experimental.pallas import tpu as pltpu
from jax.sharding import Mesh, PartitionSpec as P

TAYLOR = 5
field_scale = 0.4
f32, bf16 = jnp.float32, jnp.bfloat16

CHOL = ("zl", "core")
WALK = ("y", "x", "zh")
PLANE = ("y", "x")
RING = ("zh", "zl")


def iota(shape, dim):
    return lax.broadcasted_iota(jnp.int32, shape, dim)


def plane_index():
    return lax.axis_index("y") * 4 + lax.axis_index("x")


def chol_index():
    return lax.axis_index("zl") * 2 + lax.axis_index("core")


def pack_kernel(orb_hbm, chol_hbm, out_ref, orb_ref, chol_ref, sems):
    copies = [pltpu.make_async_copy(chol_hbm, chol_ref, sems.at[0]), pltpu.make_async_copy(orb_hbm, orb_ref, sems.at[1])]
    for copy in copies:
        copy.start()
    p = plane_index()
    start = p // 2

    def block(d):
        col = pl.multiple_of(lax.rem(start + d, 8) * 128, 128)
        return chol_ref[:, pl.ds(col, 128)]

    copies[0].wait()
    for d in range(4):
        out_ref[:, 128 * d:128 * d + 128] = block(d)
    last = block(4).astype(f32)
    half = jnp.bitwise_xor(jnp.bitwise_and(p, 1), (start >= 4).astype(jnp.int32))
    last = jnp.where(half == 1, pltpu.roll(last, 64, 1), last)
    copies[1].wait()
    low = jnp.concatenate([orb_ref[...], jnp.zeros((64, 56), f32)], axis=1)
    top, bottom = low[0:32], low[32:64]
    lane = iota((32, 128), 1)
    out_ref[:, 512:640] = jnp.where(lane < 64, last, pltpu.roll(bottom[:, 128:256], 64, 1)).astype(bf16)
    out_ref[:, 640:768] = top[:, 0:128].astype(bf16)
    out_ref[:, 768:896] = bottom[:, 0:128].astype(bf16)
    ends = jnp.where(lane < 72, top[:, 128:256], pltpu.roll(bottom[:, 128:256], 8, 1))
    out_ref[:, 896:976] = ends[:, 0:80].astype(bf16)


def select_kernel(ring_ref, own_ref, send_ref):
    k, h = lax.axis_index("core"), lax.axis_index("zh")
    lane = iota((32, 128), 1)
    for j in range(8):
        for half, target in ((k, own_ref), (1 - k, send_ref)):
            target[j, :, 0:512] = ring_ref[half, j, :, 0:512]
            tail = ring_ref[half, j, :, 512:640].astype(f32)
            target[j, :, 512:640] = jnp.where(lane < 64, tail, 0.0).astype(bf16)
        middle = ring_ref[h, j, :, 512:640].astype(f32)
        ends = jnp.concatenate([ring_ref[h, j, :, 896:976].astype(f32), jnp.zeros((32, 48), f32)], axis=1)
        top = jnp.where(lane < 72, ends, 0.0).astype(bf16)
        bottom = jnp.where(lane < 64, pltpu.roll(middle, 64, 1), jnp.where(lane < 72, pltpu.roll(ends, 120, 1), 0.0))
        bottom = bottom.astype(bf16)
        for target in (own_ref, send_ref):
            target[j, :, 640:768] = ring_ref[h, j, :, 640:768]
            target[j, :, 768:896] = top
            target[j, :, 896:1024] = ring_ref[h, j, :, 768:896]
            target[j, :, 1024:1152] = bottom


def bias_kernel(field_ref, own_ref, got_ref, inv_ref, hr_ref, term_ref, out_ref, inv_low, inv_high):
    k = lax.axis_index("core")
    for j in range(8):
        for source, core in ((own_ref, k), (got_ref, 1 - k)):
            row = pl.multiple_of((2 * j + core) * 64, 64)
            term_ref[pl.ds(row, 32), :] = source[j, :, 640:896]
            term_ref[pl.ds(row + 32, 32), :] = source[j, :, 896:1152]
    inverse = inv_ref[...]
    wide = jnp.concatenate([inverse, jnp.zeros((200, 56), f32)], axis=1)
    full = jnp.concatenate([wide, jnp.zeros((56, 256), f32)], axis=0)
    high = full.astype(bf16)
    inv_high[...] = high
    inv_low[...] = (full - high.astype(f32)).astype(bf16)
    term = term_ref[...]
    theta = jnp.dot(term, inv_high[...], preferred_element_type=f32)
    theta += jnp.dot(term, inv_low[...], preferred_element_type=f32)
    theta_high = theta.astype(bf16)
    theta_low = (theta - theta_high.astype(f32)).astype(bf16)
    rotated = hr_ref[...]
    product = jnp.dot(rotated, theta_high, preferred_element_type=f32)
    product += jnp.dot(rotated, theta_low, preferred_element_type=f32)
    diagonal = jnp.where(iota((200, 256), 0) == iota((200, 256), 1), product, 0.0)
    raw_bias = jnp.sum(jnp.sum(diagonal, axis=0, keepdims=True), axis=1, keepdims=True)
    shifted = field_scale * (field_ref[0, 0] - jnp.clip(raw_bias, -1.0, 1.0))
    row = jnp.where(iota((1, 128), 1) == plane_index(), shifted, 0.0)
    for j in range(16):
        out_ref[j] = row


def sum_kernel(in_ref, out_ref):
    row = jnp.sum(in_ref[...], axis=0)
    for j in range(16):
        out_ref[j] = row


def operator_kernel(in_ref, own_ref, got_ref, out_ref):
    k = lax.axis_index("core")
    shifted = in_ref[:, 0, :]
    by_walker = jnp.concatenate([shifted, jnp.zeros((112, 128), f32)], axis=0).T
    high = by_walker.astype(bf16)
    rest = (by_walker - high.astype(f32)).astype(bf16)
    g, q = iota((128, 512), 0), iota((128, 512), 1) >> 5
    vector = 2 * (q & 7) + jnp.where(q < 8, k, 1 - k)
    pick = jnp.where(g == vector, 1.0, 0.0).astype(bf16)
    walkers = jnp.where((iota((512, 128), 0) >> 5) == iota((512, 128), 1), 1.0, 0.0).astype(bf16)
    same = (iota((512, 512), 0) & 31) == (iota((512, 512), 1) & 31)

    def weights(part):
        spread = jnp.dot(part, pick, preferred_element_type=f32).astype(bf16)
        full = jnp.dot(walkers, spread, preferred_element_type=f32)
        return jnp.where(same, full, 0.0).astype(bf16)

    w_high, w_rest = weights(high), weights(rest)
    own = own_ref[:, :, 0:640].reshape(256, 640)
    got = got_ref[:, :, 0:640].reshape(256, 640)
    vectors = jnp.concatenate([own, got], axis=0)
    for i in range(2):
        rows = slice(256 * i, 256 * i + 256)
        value = jnp.dot(w_rest[rows], vectors, preferred_element_type=f32)
        value += jnp.dot(w_high[rows], vectors, preferred_element_type=f32)
        out_ref[rows, :] = value.astype(bf16)


def taylor_kernel(orb_ref, mine_ref, other_ref, first_ref, out_ref, op, tail, term_a, term_b):
    k = lax.axis_index("core")
    for p in range(16):
        here = pl.multiple_of(64 * p + 32 * k, 32)
        there = pl.multiple_of(64 * p + 32 * (1 - k), 32)
        for row, source in ((here, mine_ref), (there, other_ref)):
            for d in range(4):
                col = ((p // 2 + d) % 8) * 128
                op[pl.ds(row, 32), col:col + 128] = source[p, :, 128 * d:128 * d + 128]
            tail[pl.ds(row, 32), :] = source[p, :, 512:640].astype(f32)
    for i in range(8):
        for d in range(1, 4):
            j = (i + d) % 8
            block = op[128 * i:128 * i + 128, 128 * j:128 * j + 128].astype(f32)
            op[128 * j:128 * j + 128, 128 * i:128 * i + 128] = block.T.astype(bf16)
    left = iota((64, 128), 1) < 64
    for i in range(4):
        j = i + 4
        near = tail[128 * i:128 * i + 128, :]
        far = tail[128 * j:128 * j + 128, :].T[0:64]
        top = jnp.where(left, near[0:64], far)
        bottom = jnp.where(left, far, pltpu.roll(near[64:128], 64, 1))
        block = jnp.concatenate([top, bottom], axis=0)
        op[128 * i:128 * i + 128, 128 * j:128 * j + 128] = block.astype(bf16)
        op[128 * j:128 * j + 128, 128 * i:128 * i + 128] = block.T.astype(bf16)
    own = pl.multiple_of(chol_index() * 64, 64)
    own_rows = op[pl.ds(own, 64), :]
    total = jnp.zeros((64, 256), f32)
    now, later, spare = first_ref, term_a, term_b
    for degree in range(1, TAYLOR + 1):
        term = now[...]
        total += jnp.dot(own_rows, term, preferred_element_type=f32) * (1.0 / degree)
        if degree < TAYLOR:
            for i in range(4):
                image = jnp.dot(op[256 * i:256 * i + 256, :], term, preferred_element_type=f32)
                later[256 * i:256 * i + 256, :] = (image * (1.0 / degree)).astype(bf16)
            now, later, spare = later, spare, later
    out_ref[...] = orb_ref[...] + total[:, :200]


def call(body, outs, *args, scratch=(), smem=0, hbm=(), grant=40):
    vmem = pl.BlockSpec(memory_space=pltpu.VMEM)
    specs = [pl.BlockSpec(memory_space=pltpu.SMEM)] * smem + [vmem] * (len(args) - smem)
    for i in hbm:
        specs[i] = pl.BlockSpec(memory_space=pl.ANY)
    many = isinstance(outs, (list, tuple))
    return pl.pallas_call(
        body,
        out_shape=outs,
        in_specs=specs,
        out_specs=[vmem] * len(outs) if many else vmem,
        scratch_shapes=list(scratch),
        compiler_params=pltpu.CompilerParams(vmem_limit_bytes=grant * 2**20),
    )(*args)


def shape(dims, dtype):
    return jax.ShapeDtypeStruct(dims, dtype)


def exchange(value, axes):
    return lax.all_to_all(value, axes, 0, 0, tiled=True)


def shards(orbitals, inverse_intersection, half_rotated, chol_full, fields):
    orb = orbitals[0]
    packed = call(
        pack_kernel, shape((32, 976), bf16), orb, chol_full[0],
        scratch=[pltpu.VMEM((64, 200), f32), pltpu.VMEM((32, 1024), bf16), pltpu.SemaphoreType.DMA((2,))],
        hbm=(0, 1), grant=60,
    )
    ring = lax.all_gather(packed, RING, axis=0, tiled=True)
    own, send = call(select_kernel, [shape((8, 32, 1152), bf16)] * 2, ring.reshape(2, 8, 32, 976))
    swap_core = [(0, 1), (1, 0)]
    got = lax.ppermute(send, "core", swap_core)
    first, partial = call(
        bias_kernel, [shape((1024, 256), bf16), shape((16, 1, 128), f32)],
        fields, own, got, inverse_intersection[0], half_rotated[0],
        scratch=[pltpu.VMEM((256, 256), bf16), pltpu.VMEM((256, 256), bf16)], smem=1,
    )
    in_plane = exchange(partial, PLANE)
    summed = call(sum_kernel, shape((16, 1, 128), f32), in_plane)
    everywhere = exchange(summed, CHOL)
    pieces = call(operator_kernel, shape((512, 640), bf16), everywhere, own, got)
    mine = exchange(pieces.reshape(16, 32, 640), PLANE)
    other = lax.ppermute(mine, "core", swap_core)
    out = call(
        taylor_kernel, shape((64, 200), f32), orb, mine, other, first,
        scratch=[pltpu.VMEM((1024, 1024), bf16), pltpu.VMEM((1024, 128), f32),
                 pltpu.VMEM((1024, 256), bf16), pltpu.VMEM((1024, 256), bf16)],
    )
    return out[None]


def solution(mesh):
    fine = Mesh(mesh.devices.reshape(8, 2, 4, 4, 2), ("zl", "core", "y", "x", "zh"))
    return jax.shard_map(
        shards,
        mesh=fine,
        in_specs=(
            P(WALK, CHOL, None),
            P(WALK, None, None),
            P(CHOL, None, None),
            P(CHOL, WALK, None),
            P(CHOL, WALK),
        ),
        out_specs=P(WALK, CHOL, None),
        check_vma=False,
    )
```

```python
import jax
import jax.numpy as jnp
from jax import lax
from jax.experimental import pallas as pl
from jax.experimental.pallas import tpu as pltpu
from jax.sharding import Mesh, PartitionSpec as P

TAYLOR = 5
field_scale = 0.4
f32, bf16 = jnp.float32, jnp.bfloat16

CHOL = ("zl", "core")
WALK = ("y", "x", "zh")
PLANE = ("y", "x")
RING = ("zh", "zl")


def iota(shape, dim):
    return lax.broadcasted_iota(jnp.int32, shape, dim)


def plane_index():
    return lax.axis_index("y") * 4 + lax.axis_index("x")


def chol_index():
    return lax.axis_index("zl") * 2 + lax.axis_index("core")


def pack_kernel(orb_hbm, chol_hbm, out_ref, orb_ref, chol_ref, sems):
    copies = [pltpu.make_async_copy(chol_hbm, chol_ref, sems.at[0]), pltpu.make_async_copy(orb_hbm, orb_ref, sems.at[1])]
    for copy in copies:
        copy.start()
    p = plane_index()
    start = p // 2

    def block(d):
        col = pl.multiple_of(lax.rem(start + d, 8) * 128, 128)
        return chol_ref[:, pl.ds(col, 128)]

    copies[0].wait()
    for d in range(4):
        out_ref[:, 128 * d:128 * d + 128] = block(d)
    last = block(4).astype(f32)
    half = jnp.bitwise_xor(jnp.bitwise_and(p, 1), (start >= 4).astype(jnp.int32))
    last = jnp.where(half == 1, pltpu.roll(last, 64, 1), last)
    copies[1].wait()
    low = jnp.concatenate([orb_ref[...], jnp.zeros((64, 56), f32)], axis=1)
    top, bottom = low[0:32], low[32:64]
    lane = iota((32, 128), 1)
    out_ref[:, 512:640] = jnp.where(lane < 64, last, pltpu.roll(bottom[:, 128:256], 64, 1)).astype(bf16)
    out_ref[:, 640:768] = top[:, 0:128].astype(bf16)
    out_ref[:, 768:896] = bottom[:, 0:128].astype(bf16)
    ends = jnp.where(lane < 72, top[:, 128:256], pltpu.roll(bottom[:, 128:256], 8, 1))
    out_ref[:, 896:976] = ends[:, 0:80].astype(bf16)


def select_kernel(ring_ref, own_ref, send_ref):
    k, h = lax.axis_index("core"), lax.axis_index("zh")
    lane = iota((32, 128), 1)
    for j in range(8):
        for half, target in ((k, own_ref), (1 - k, send_ref)):
            target[j, :, 0:512] = ring_ref[half, j, :, 0:512]
            tail = ring_ref[half, j, :, 512:640].astype(f32)
            target[j, :, 512:640] = jnp.where(lane < 64, tail, 0.0).astype(bf16)
        middle = ring_ref[h, j, :, 512:640].astype(f32)
        ends = jnp.concatenate([ring_ref[h, j, :, 896:976].astype(f32), jnp.zeros((32, 48), f32)], axis=1)
        top = jnp.where(lane < 72, ends, 0.0).astype(bf16)
        bottom = jnp.where(lane < 64, pltpu.roll(middle, 64, 1), jnp.where(lane < 72, pltpu.roll(ends, 120, 1), 0.0))
        bottom = bottom.astype(bf16)
        for target in (own_ref, send_ref):
            target[j, :, 640:768] = ring_ref[h, j, :, 640:768]
            target[j, :, 768:896] = top
            target[j, :, 896:1024] = ring_ref[h, j, :, 768:896]
            target[j, :, 1024:1152] = bottom


def bias_kernel(field_ref, own_ref, got_ref, inv_ref, hr_ref, term_ref, out_ref, inv_low, inv_high):
    k = lax.axis_index("core")
    for j in range(8):
        for source, core in ((own_ref, k), (got_ref, 1 - k)):
            row = pl.multiple_of((2 * j + core) * 64, 64)
            term_ref[pl.ds(row, 32), :] = source[j, :, 640:896]
            term_ref[pl.ds(row + 32, 32), :] = source[j, :, 896:1152]
    inverse = inv_ref[...]
    wide = jnp.concatenate([inverse, jnp.zeros((200, 56), f32)], axis=1)
    full = jnp.concatenate([wide, jnp.zeros((56, 256), f32)], axis=0)
    high = full.astype(bf16)
    inv_high[...] = high
    inv_low[...] = (full - high.astype(f32)).astype(bf16)
    term = term_ref[...]
    theta = jnp.dot(term, inv_high[...], preferred_element_type=f32)
    theta += jnp.dot(term, inv_low[...], preferred_element_type=f32)
    theta_high = theta.astype(bf16)
    theta_low = (theta - theta_high.astype(f32)).astype(bf16)
    rotated = hr_ref[...]
    product = jnp.dot(rotated, theta_high, preferred_element_type=f32)
    product += jnp.dot(rotated, theta_low, preferred_element_type=f32)
    diagonal = jnp.where(iota((200, 256), 0) == iota((200, 256), 1), product, 0.0)
    raw_bias = jnp.sum(jnp.sum(diagonal, axis=0, keepdims=True), axis=1, keepdims=True)
    shifted = field_scale * (field_ref[0, 0] - jnp.clip(raw_bias, -1.0, 1.0))
    row = jnp.where(iota((1, 128), 1) == chol_index(), shifted, 0.0)
    for j in range(16):
        out_ref[j] = row


def sum_kernel(in_ref, out_ref):
    row = jnp.sum(in_ref[...], axis=0)
    for j in range(16):
        out_ref[j] = row


def operator_kernel(in_ref, own_ref, got_ref, out_ref):
    k = lax.axis_index("core")
    by_walker = jnp.concatenate([in_ref[:, 0, :], jnp.zeros((112, 128), f32)], axis=0)
    high = by_walker.astype(bf16)
    rest = (by_walker - high.astype(f32)).astype(bf16)
    g, q = iota((128, 512), 0), iota((128, 512), 1) >> 5
    vector = 2 * (q & 7) + jnp.where(q < 8, k, 1 - k)
    pick = jnp.where(g == vector, 1.0, 0.0).astype(bf16)
    walkers = jnp.where((iota((512, 128), 0) >> 5) == iota((512, 128), 1), 1.0, 0.0).astype(bf16)
    same = (iota((512, 512), 0) & 31) == (iota((512, 512), 1) & 31)

    def weights(part):
        spread = jnp.dot(part, pick, preferred_element_type=f32).astype(bf16)
        full = jnp.dot(walkers, spread, preferred_element_type=f32)
        return jnp.where(same, full, 0.0).astype(bf16)

    w_high, w_rest = weights(high), weights(rest)
    own = own_ref[:, :, 0:640].reshape(256, 640)
    got = got_ref[:, :, 0:640].reshape(256, 640)
    vectors = jnp.concatenate([own, got], axis=0)
    for i in range(2):
        rows = slice(256 * i, 256 * i + 256)
        value = jnp.dot(w_rest[rows], vectors, preferred_element_type=f32)
        value += jnp.dot(w_high[rows], vectors, preferred_element_type=f32)
        out_ref[rows, :] = value.astype(bf16)


def taylor_kernel(orb_ref, mine_ref, other_ref, first_ref, out_ref, op, tail, term_a, term_b):
    k = lax.axis_index("core")
    for p in range(16):
        here = pl.multiple_of(64 * p + 32 * k, 32)
        there = pl.multiple_of(64 * p + 32 * (1 - k), 32)
        for row, source in ((here, mine_ref), (there, other_ref)):
            for d in range(4):
                col = ((p // 2 + d) % 8) * 128
                op[pl.ds(row, 32), col:col + 128] = source[p, :, 128 * d:128 * d + 128]
            tail[pl.ds(row, 32), :] = source[p, :, 512:640].astype(f32)
    for i in range(8):
        for d in range(1, 4):
            j = (i + d) % 8
            block = op[128 * i:128 * i + 128, 128 * j:128 * j + 128].astype(f32)
            op[128 * j:128 * j + 128, 128 * i:128 * i + 128] = block.T.astype(bf16)
    left = iota((64, 128), 1) < 64
    for i in range(4):
        j = i + 4
        near = tail[128 * i:128 * i + 128, :]
        far = tail[128 * j:128 * j + 128, :].T[0:64]
        top = jnp.where(left, near[0:64], far)
        bottom = jnp.where(left, far, pltpu.roll(near[64:128], 64, 1))
        block = jnp.concatenate([top, bottom], axis=0)
        op[128 * i:128 * i + 128, 128 * j:128 * j + 128] = block.astype(bf16)
        op[128 * j:128 * j + 128, 128 * i:128 * i + 128] = block.T.astype(bf16)
    own = pl.multiple_of(chol_index() * 64, 64)
    own_rows = op[pl.ds(own, 64), :]
    total = jnp.zeros((64, 256), f32)
    now, later, spare = first_ref, term_a, term_b
    for degree in range(1, TAYLOR + 1):
        term = now[...]
        total += jnp.dot(own_rows, term, preferred_element_type=f32) * (1.0 / degree)
        if degree < TAYLOR:
            for i in range(4):
                image = jnp.dot(op[256 * i:256 * i + 256, :], term, preferred_element_type=f32)
                later[256 * i:256 * i + 256, :] = (image * (1.0 / degree)).astype(bf16)
            now, later, spare = later, spare, later
    out_ref[...] = orb_ref[...] + total[:, :200]


def call(body, outs, *args, scratch=(), smem=0, hbm=(), grant=40):
    vmem = pl.BlockSpec(memory_space=pltpu.VMEM)
    specs = [pl.BlockSpec(memory_space=pltpu.SMEM)] * smem + [vmem] * (len(args) - smem)
    for i in hbm:
        specs[i] = pl.BlockSpec(memory_space=pl.ANY)
    many = isinstance(outs, (list, tuple))
    return pl.pallas_call(
        body,
        out_shape=outs,
        in_specs=specs,
        out_specs=[vmem] * len(outs) if many else vmem,
        scratch_shapes=list(scratch),
        compiler_params=pltpu.CompilerParams(vmem_limit_bytes=grant * 2**20),
    )(*args)


def shape(dims, dtype):
    return jax.ShapeDtypeStruct(dims, dtype)


def exchange(value, axes):
    return lax.all_to_all(value, axes, 0, 0, tiled=True)


def shards(orbitals, inverse_intersection, half_rotated, chol_full, fields):
    orb = orbitals[0]
    packed = call(
        pack_kernel, shape((32, 976), bf16), orb, chol_full[0],
        scratch=[pltpu.VMEM((64, 200), f32), pltpu.VMEM((32, 1024), bf16), pltpu.SemaphoreType.DMA((2,))],
        hbm=(0, 1), grant=60,
    )
    ring = lax.all_gather(packed, RING, axis=0, tiled=True)
    own, send = call(select_kernel, [shape((8, 32, 1152), bf16)] * 2, ring.reshape(2, 8, 32, 976))
    swap_core = [(0, 1), (1, 0)]
    got = lax.ppermute(send, "core", swap_core)
    first, partial = call(
        bias_kernel, [shape((1024, 256), bf16), shape((16, 1, 128), f32)],
        fields, own, got, inverse_intersection[0], half_rotated[0],
        scratch=[pltpu.VMEM((256, 256), bf16), pltpu.VMEM((256, 256), bf16)], smem=1,
    )
    along_z = exchange(partial, CHOL)
    summed = call(sum_kernel, shape((16, 1, 128), f32), along_z)
    everywhere = exchange(summed, PLANE)
    pieces = call(operator_kernel, shape((512, 640), bf16), everywhere, own, got)
    mine = exchange(pieces.reshape(16, 32, 640), PLANE)
    other = lax.ppermute(mine, "core", swap_core)
    out = call(
        taylor_kernel, shape((64, 200), f32), orb, mine, other, first,
        scratch=[pltpu.VMEM((1024, 1024), bf16), pltpu.VMEM((1024, 128), f32),
                 pltpu.VMEM((1024, 256), bf16), pltpu.VMEM((1024, 256), bf16)],
    )
    return out[None]


def solution(mesh):
    fine = Mesh(mesh.devices.reshape(8, 2, 4, 4, 2), ("zl", "core", "y", "x", "zh"))
    return jax.shard_map(
        shards,
        mesh=fine,
        in_specs=(
            P(WALK, CHOL, None),
            P(WALK, None, None),
            P(CHOL, None, None),
            P(CHOL, WALK, None),
            P(CHOL, WALK),
        ),
        out_specs=P(WALK, CHOL, None),
        check_vma=False,
    )
```

```python
import jax
import jax.numpy as jnp
from jax import lax
from jax.experimental import pallas as pl
from jax.experimental.pallas import tpu as pltpu
from jax.sharding import Mesh, PartitionSpec as P

TAYLOR = 5
field_scale = 0.4
f32, bf16 = jnp.float32, jnp.bfloat16

CHOL = ("zl", "core")
WALK = ("y", "x", "zh")
PLANE = ("y", "x")
RING = ("zh", "zl")


def iota(shape, dim):
    return lax.broadcasted_iota(jnp.int32, shape, dim)


def plane_index():
    return lax.axis_index("y") * 4 + lax.axis_index("x")


def chol_index():
    return lax.axis_index("zl") * 2 + lax.axis_index("core")


def pack_kernel(orb_hbm, chol_hbm, out_ref, orb_ref, chol_ref, sems):
    copies = [pltpu.make_async_copy(chol_hbm, chol_ref, sems.at[0]), pltpu.make_async_copy(orb_hbm, orb_ref, sems.at[1])]
    for copy in copies:
        copy.start()
    p = plane_index()
    start = p // 2

    def block(d):
        col = pl.multiple_of(lax.rem(start + d, 8) * 128, 128)
        return chol_ref[:, pl.ds(col, 128)]

    copies[0].wait()
    for d in range(4):
        out_ref[:, 128 * d:128 * d + 128] = block(d)
    last = block(4).astype(f32)
    half = jnp.bitwise_xor(jnp.bitwise_and(p, 1), (start >= 4).astype(jnp.int32))
    last = jnp.where(half == 1, pltpu.roll(last, 64, 1), last)
    copies[1].wait()
    low = jnp.concatenate([orb_ref[...], jnp.zeros((64, 56), f32)], axis=1)
    top, bottom = low[0:32], low[32:64]
    lane = iota((32, 128), 1)
    out_ref[:, 512:640] = jnp.where(lane < 64, last, pltpu.roll(bottom[:, 128:256], 64, 1)).astype(bf16)
    out_ref[:, 640:768] = top[:, 0:128].astype(bf16)
    out_ref[:, 768:896] = bottom[:, 0:128].astype(bf16)
    ends = jnp.where(lane < 72, top[:, 128:256], pltpu.roll(bottom[:, 128:256], 8, 1))
    out_ref[:, 896:976] = ends[:, 0:80].astype(bf16)


def select_kernel(ring_ref, own_ref, send_ref):
    k, h = lax.axis_index("core"), lax.axis_index("zh")
    lane = iota((32, 128), 1)
    for j in range(8):
        for half, target in ((k, own_ref), (1 - k, send_ref)):
            target[j, :, 0:512] = ring_ref[half, j, :, 0:512]
            tail = ring_ref[half, j, :, 512:640].astype(f32)
            target[j, :, 512:640] = jnp.where(lane < 64, tail, 0.0).astype(bf16)
        middle = ring_ref[h, j, :, 512:640].astype(f32)
        ends = jnp.concatenate([ring_ref[h, j, :, 896:976].astype(f32), jnp.zeros((32, 48), f32)], axis=1)
        top = jnp.where(lane < 72, ends, 0.0).astype(bf16)
        bottom = jnp.where(lane < 64, pltpu.roll(middle, 64, 1), jnp.where(lane < 72, pltpu.roll(ends, 120, 1), 0.0))
        bottom = bottom.astype(bf16)
        for target in (own_ref, send_ref):
            target[j, :, 640:768] = ring_ref[h, j, :, 640:768]
            target[j, :, 768:896] = top
            target[j, :, 896:1024] = ring_ref[h, j, :, 768:896]
            target[j, :, 1024:1152] = bottom


def bias_kernel(field_ref, own_ref, got_ref, inv_ref, hr_ref, term_ref, out_ref, inv_low, inv_high):
    k = lax.axis_index("core")
    for j in range(8):
        for source, core in ((own_ref, k), (got_ref, 1 - k)):
            row = pl.multiple_of((2 * j + core) * 64, 64)
            term_ref[pl.ds(row, 32), :] = source[j, :, 640:896]
            term_ref[pl.ds(row + 32, 32), :] = source[j, :, 896:1152]
    inverse = inv_ref[...]
    wide = jnp.concatenate([inverse, jnp.zeros((200, 56), f32)], axis=1)
    full = jnp.concatenate([wide, jnp.zeros((56, 256), f32)], axis=0)
    high = full.astype(bf16)
    inv_high[...] = high
    inv_low[...] = (full - high.astype(f32)).astype(bf16)
    term = term_ref[...]
    theta = jnp.dot(term, inv_high[...], preferred_element_type=f32)
    theta += jnp.dot(term, inv_low[...], preferred_element_type=f32)
    theta_high = theta.astype(bf16)
    theta_low = (theta - theta_high.astype(f32)).astype(bf16)
    rotated = hr_ref[...]
    product = jnp.dot(rotated, theta_high, preferred_element_type=f32)
    product += jnp.dot(rotated, theta_low, preferred_element_type=f32)
    diagonal = jnp.where(iota((200, 256), 0) == iota((200, 256), 1), product, 0.0)
    raw_bias = jnp.sum(jnp.sum(diagonal, axis=0, keepdims=True), axis=1, keepdims=True)
    shifted = field_scale * (field_ref[0, 0] - jnp.clip(raw_bias, -1.0, 1.0))
    row = jnp.where(iota((1, 128), 1) == chol_index(), shifted, 0.0)
    for j in range(16):
        out_ref[j] = row


def sum_kernel(in_ref, out_ref):
    row = jnp.sum(in_ref[...], axis=0)
    for j in range(16):
        out_ref[j] = row


def operator_kernel(in_ref, own_ref, got_ref, out_ref):
    k = lax.axis_index("core")
    by_walker = jnp.concatenate([in_ref[:, 0, :], jnp.zeros((112, 128), f32)], axis=0)
    high = by_walker.astype(bf16)
    rest = (by_walker - high.astype(f32)).astype(bf16)
    g, q = iota((128, 512), 0), iota((128, 512), 1) >> 5
    vector = 2 * (q & 7) + jnp.where(q < 8, k, 1 - k)
    pick = jnp.where(g == vector, 1.0, 0.0).astype(bf16)
    walkers = jnp.where((iota((512, 128), 0) >> 5) == iota((512, 128), 1), 1.0, 0.0).astype(bf16)
    same = (iota((512, 512), 0) & 31) == (iota((512, 512), 1) & 31)

    def weights(part):
        spread = jnp.dot(part, pick, preferred_element_type=f32).astype(bf16)
        full = jnp.dot(walkers, spread, preferred_element_type=f32)
        return jnp.where(same, full, 0.0).astype(bf16)

    w_high, w_rest = weights(high), weights(rest)
    own = own_ref[:, :, 0:640].reshape(256, 640)
    got = got_ref[:, :, 0:640].reshape(256, 640)
    vectors = jnp.concatenate([own, got], axis=0)
    for i in range(2):
        rows = slice(256 * i, 256 * i + 256)
        value = jnp.dot(w_rest[rows], vectors, preferred_element_type=f32)
        value += jnp.dot(w_high[rows], vectors, preferred_element_type=f32)
        out_ref[rows, :] = value.astype(bf16)


def taylor_kernel(orb_ref, mine_ref, other_ref, first_ref, out_ref, op, tail):
    k = lax.axis_index("core")
    for p in range(16):
        here = pl.multiple_of(64 * p + 32 * k, 32)
        there = pl.multiple_of(64 * p + 32 * (1 - k), 32)
        for row, source in ((here, mine_ref), (there, other_ref)):
            for d in range(4):
                col = ((p // 2 + d) % 8) * 128
                op[pl.ds(row, 32), col:col + 128] = source[p, :, 128 * d:128 * d + 128]
            tail[pl.ds(row, 32), :] = source[p, :, 512:640].astype(f32)
    for i in range(8):
        for d in range(1, 4):
            j = (i + d) % 8
            block = op[128 * i:128 * i + 128, 128 * j:128 * j + 128].astype(f32)
            op[128 * j:128 * j + 128, 128 * i:128 * i + 128] = block.T.astype(bf16)
    left = iota((64, 128), 1) < 64
    for i in range(4):
        j = i + 4
        near = tail[128 * i:128 * i + 128, :]
        far = tail[128 * j:128 * j + 128, :].T[0:64]
        top = jnp.where(left, near[0:64], far)
        bottom = jnp.where(left, far, pltpu.roll(near[64:128], 64, 1))
        block = jnp.concatenate([top, bottom], axis=0)
        op[128 * i:128 * i + 128, 128 * j:128 * j + 128] = block.astype(bf16)
        op[128 * j:128 * j + 128, 128 * i:128 * i + 128] = block.T.astype(bf16)
    own = pl.multiple_of(chol_index() * 64, 64)
    own_rows = op[pl.ds(own, 64), :]
    power, share = own_rows, 1.0
    series = power.astype(f32)
    for degree in range(2, TAYLOR + 1):
        product = jnp.dot(power, op[...], preferred_element_type=f32)
        share = share / degree
        series += product * share
        power = product.astype(bf16)
    high = series.astype(bf16)
    rest = (series - high.astype(f32)).astype(bf16)
    first = first_ref[...]
    total = jnp.dot(rest, first, preferred_element_type=f32)
    total += jnp.dot(high, first, preferred_element_type=f32)
    out_ref[...] = orb_ref[...] + total[:, :200]


def call(body, outs, *args, scratch=(), smem=0, hbm=(), grant=40):
    vmem = pl.BlockSpec(memory_space=pltpu.VMEM)
    specs = [pl.BlockSpec(memory_space=pltpu.SMEM)] * smem + [vmem] * (len(args) - smem)
    for i in hbm:
        specs[i] = pl.BlockSpec(memory_space=pl.ANY)
    many = isinstance(outs, (list, tuple))
    return pl.pallas_call(
        body,
        out_shape=outs,
        in_specs=specs,
        out_specs=[vmem] * len(outs) if many else vmem,
        scratch_shapes=list(scratch),
        compiler_params=pltpu.CompilerParams(vmem_limit_bytes=grant * 2**20),
    )(*args)


def shape(dims, dtype):
    return jax.ShapeDtypeStruct(dims, dtype)


def exchange(value, axes):
    return lax.all_to_all(value, axes, 0, 0, tiled=True)


def shards(orbitals, inverse_intersection, half_rotated, chol_full, fields):
    orb = orbitals[0]
    packed = call(
        pack_kernel, shape((32, 976), bf16), orb, chol_full[0],
        scratch=[pltpu.VMEM((64, 200), f32), pltpu.VMEM((32, 1024), bf16), pltpu.SemaphoreType.DMA((2,))],
        hbm=(0, 1), grant=60,
    )
    ring = lax.all_gather(packed, RING, axis=0, tiled=True)
    own, send = call(select_kernel, [shape((8, 32, 1152), bf16)] * 2, ring.reshape(2, 8, 32, 976))
    swap_core = [(0, 1), (1, 0)]
    got = lax.ppermute(send, "core", swap_core)
    first, partial = call(
        bias_kernel, [shape((1024, 256), bf16), shape((16, 1, 128), f32)],
        fields, own, got, inverse_intersection[0], half_rotated[0],
        scratch=[pltpu.VMEM((256, 256), bf16), pltpu.VMEM((256, 256), bf16)], smem=1,
    )
    along_z = exchange(partial, CHOL)
    summed = call(sum_kernel, shape((16, 1, 128), f32), along_z)
    everywhere = exchange(summed, PLANE)
    pieces = call(operator_kernel, shape((512, 640), bf16), everywhere, own, got)
    mine = exchange(pieces.reshape(16, 32, 640), PLANE)
    other = lax.ppermute(mine, "core", swap_core)
    out = call(
        taylor_kernel, shape((64, 200), f32), orb, mine, other, first,
        scratch=[pltpu.VMEM((1024, 1024), bf16), pltpu.VMEM((1024, 128), f32)],
    )
    return out[None]


def solution(mesh):
    fine = Mesh(mesh.devices.reshape(8, 2, 4, 4, 2), ("zl", "core", "y", "x", "zh"))
    return jax.shard_map(
        shards,
        mesh=fine,
        in_specs=(
            P(WALK, CHOL, None),
            P(WALK, None, None),
            P(CHOL, None, None),
            P(CHOL, WALK, None),
            P(CHOL, WALK),
        ),
        out_specs=P(WALK, CHOL, None),
        check_vma=False,
    )
```

```python
import jax
import jax.numpy as jnp
from jax import lax
from jax.experimental import pallas as pl
from jax.experimental.pallas import tpu as pltpu
from jax.sharding import Mesh, PartitionSpec as P

TAYLOR = 5
field_scale = 0.4
f32, bf16 = jnp.float32, jnp.bfloat16

CHOL = ("zl", "core")
WALK = ("y", "x", "zh")
PLANE = ("y", "x")
RING = ("zh", "zl")


def iota(shape, dim):
    return lax.broadcasted_iota(jnp.int32, shape, dim)


def plane_index():
    return lax.axis_index("y") * 4 + lax.axis_index("x")


def chol_index():
    return lax.axis_index("zl") * 2 + lax.axis_index("core")


def pack_kernel(orb_hbm, chol_hbm, out_ref, orb_ref, chol_ref, sems):
    copies = [pltpu.make_async_copy(chol_hbm, chol_ref, sems.at[0]), pltpu.make_async_copy(orb_hbm, orb_ref, sems.at[1])]
    for copy in copies:
        copy.start()
    p = plane_index()
    start = p // 2

    def block(d):
        col = pl.multiple_of(lax.rem(start + d, 8) * 128, 128)
        return chol_ref[:, pl.ds(col, 128)]

    copies[0].wait()
    for d in range(4):
        out_ref[:, 128 * d:128 * d + 128] = block(d)
    last = block(4).astype(f32)
    half = jnp.bitwise_xor(jnp.bitwise_and(p, 1), (start >= 4).astype(jnp.int32))
    last = jnp.where(half == 1, pltpu.roll(last, 64, 1), last)
    copies[1].wait()
    low = jnp.concatenate([orb_ref[...], jnp.zeros((64, 56), f32)], axis=1)
    top, bottom = low[0:32], low[32:64]
    lane = iota((32, 128), 1)
    out_ref[:, 512:640] = jnp.where(lane < 64, last, pltpu.roll(bottom[:, 128:256], 64, 1)).astype(bf16)
    out_ref[:, 640:768] = top[:, 0:128].astype(bf16)
    out_ref[:, 768:896] = bottom[:, 0:128].astype(bf16)
    ends = jnp.where(lane < 72, top[:, 128:256], pltpu.roll(bottom[:, 128:256], 8, 1))
    out_ref[:, 896:976] = ends[:, 0:80].astype(bf16)


def select_kernel(ring_ref, own_ref, send_ref):
    k, h = lax.axis_index("core"), lax.axis_index("zh")
    lane = iota((32, 128), 1)
    for j in range(8):
        for half, target in ((k, own_ref), (1 - k, send_ref)):
            target[j, :, 0:512] = ring_ref[half, j, :, 0:512]
            tail = ring_ref[half, j, :, 512:640].astype(f32)
            target[j, :, 512:640] = jnp.where(lane < 64, tail, 0.0).astype(bf16)
        middle = ring_ref[h, j, :, 512:640].astype(f32)
        ends = jnp.concatenate([ring_ref[h, j, :, 896:976].astype(f32), jnp.zeros((32, 48), f32)], axis=1)
        top = jnp.where(lane < 72, ends, 0.0).astype(bf16)
        bottom = jnp.where(lane < 64, pltpu.roll(middle, 64, 1), jnp.where(lane < 72, pltpu.roll(ends, 120, 1), 0.0))
        bottom = bottom.astype(bf16)
        for target in (own_ref, send_ref):
            target[j, :, 640:768] = ring_ref[h, j, :, 640:768]
            target[j, :, 768:896] = top
            target[j, :, 896:1024] = ring_ref[h, j, :, 768:896]
            target[j, :, 1024:1152] = bottom


def bias_kernel(field_ref, own_ref, got_ref, inv_ref, hr_ref, term_ref, out_ref, inv_low, inv_high):
    k = lax.axis_index("core")
    for j in range(8):
        for source, core in ((own_ref, k), (got_ref, 1 - k)):
            row = pl.multiple_of((2 * j + core) * 64, 64)
            term_ref[pl.ds(row, 32), :] = source[j, :, 640:896]
            term_ref[pl.ds(row + 32, 32), :] = source[j, :, 896:1152]
    inverse = inv_ref[...]
    wide = jnp.concatenate([inverse, jnp.zeros((200, 56), f32)], axis=1)
    full = jnp.concatenate([wide, jnp.zeros((56, 256), f32)], axis=0)
    high = full.astype(bf16)
    inv_high[...] = high
    inv_low[...] = (full - high.astype(f32)).astype(bf16)
    term = term_ref[...]
    theta = jnp.dot(term, inv_high[...], preferred_element_type=f32)
    theta += jnp.dot(term, inv_low[...], preferred_element_type=f32)
    theta_high = theta.astype(bf16)
    theta_low = (theta - theta_high.astype(f32)).astype(bf16)
    rotated = hr_ref[...]
    product = jnp.dot(rotated, theta_high, preferred_element_type=f32)
    product += jnp.dot(rotated, theta_low, preferred_element_type=f32)
    diagonal = jnp.where(iota((200, 256), 0) == iota((200, 256), 1), product, 0.0)
    raw_bias = jnp.sum(jnp.sum(diagonal, axis=0, keepdims=True), axis=1, keepdims=True)
    shifted = field_scale * (field_ref[0, 0] - jnp.clip(raw_bias, -1.0, 1.0))
    row = jnp.where(iota((1, 128), 1) == chol_index(), shifted, 0.0)
    for j in range(16):
        out_ref[j] = row


def sum_kernel(in_ref, out_ref):
    row = jnp.sum(in_ref[...], axis=0)
    for j in range(16):
        out_ref[j] = row


def operator_kernel(in_ref, own_ref, got_ref, out_ref):
    k = lax.axis_index("core")
    by_walker = jnp.concatenate([in_ref[:, 0, :], jnp.zeros((112, 128), f32)], axis=0)
    high = by_walker.astype(bf16)
    rest = (by_walker - high.astype(f32)).astype(bf16)
    g, q = iota((128, 256), 0), iota((128, 256), 1) >> 4
    vector = 2 * (q & 7) + jnp.where(q < 8, k, 1 - k)
    pick = jnp.where(g == vector, 1.0, 0.0).astype(bf16)
    walkers = jnp.where((iota((256, 128), 0) >> 4) == iota((256, 128), 1), 1.0, 0.0).astype(bf16)
    same = (iota((256, 256), 0) & 15) == (iota((256, 256), 1) & 15)

    def weights(part):
        spread = jnp.dot(part, pick, preferred_element_type=f32).astype(bf16)
        full = jnp.dot(walkers, spread, preferred_element_type=f32)
        return jnp.where(same, full, 0.0).astype(bf16)

    w_high, w_rest = weights(high), weights(rest)
    for i in range(2):
        rows = slice(16 * i, 16 * i + 16)
        own = own_ref[:, rows, 0:640].reshape(128, 640)
        got = got_ref[:, rows, 0:640].reshape(128, 640)
        vectors = jnp.concatenate([own, got], axis=0)
        value = jnp.dot(w_rest, vectors, preferred_element_type=f32)
        value += jnp.dot(w_high, vectors, preferred_element_type=f32)
        out_ref[:, rows, :] = value.astype(bf16).reshape(16, 16, 640)


def taylor_kernel(orb_ref, mine_ref, other_ref, first_ref, out_ref, op, tail):
    k = lax.axis_index("core")
    for p in range(16):
        here = pl.multiple_of(64 * p + 32 * k, 32)
        there = pl.multiple_of(64 * p + 32 * (1 - k), 32)
        for row, source in ((here, mine_ref), (there, other_ref)):
            for d in range(4):
                col = ((p // 2 + d) % 8) * 128
                op[pl.ds(row, 32), col:col + 128] = source[p, :, 128 * d:128 * d + 128]
            tail[pl.ds(row, 32), :] = source[p, :, 512:640].astype(f32)
    for i in range(8):
        for d in range(1, 4):
            j = (i + d) % 8
            block = op[128 * i:128 * i + 128, 128 * j:128 * j + 128].astype(f32)
            op[128 * j:128 * j + 128, 128 * i:128 * i + 128] = block.T.astype(bf16)
    left = iota((64, 128), 1) < 64
    for i in range(4):
        j = i + 4
        near = tail[128 * i:128 * i + 128, :]
        far = tail[128 * j:128 * j + 128, :].T[0:64]
        top = jnp.where(left, near[0:64], far)
        bottom = jnp.where(left, far, pltpu.roll(near[64:128], 64, 1))
        block = jnp.concatenate([top, bottom], axis=0)
        op[128 * i:128 * i + 128, 128 * j:128 * j + 128] = block.astype(bf16)
        op[128 * j:128 * j + 128, 128 * i:128 * i + 128] = block.T.astype(bf16)
    own = pl.multiple_of(chol_index() * 64, 64)
    own_rows = op[pl.ds(own, 64), :]
    power, share = own_rows, 1.0
    series = power.astype(f32)
    for degree in range(2, TAYLOR + 1):
        product = jnp.dot(power, op[...], preferred_element_type=f32)
        share = share / degree
        series += product * share
        power = product.astype(bf16)
    high = series.astype(bf16)
    rest = (series - high.astype(f32)).astype(bf16)
    first = first_ref[...]
    total = jnp.dot(rest, first, preferred_element_type=f32)
    total += jnp.dot(high, first, preferred_element_type=f32)
    out_ref[...] = orb_ref[...] + total[:, :200]


def call(body, outs, *args, scratch=(), smem=0, hbm=(), grant=40):
    vmem = pl.BlockSpec(memory_space=pltpu.VMEM)
    specs = [pl.BlockSpec(memory_space=pltpu.SMEM)] * smem + [vmem] * (len(args) - smem)
    for i in hbm:
        specs[i] = pl.BlockSpec(memory_space=pl.ANY)
    many = isinstance(outs, (list, tuple))
    return pl.pallas_call(
        body,
        out_shape=outs,
        in_specs=specs,
        out_specs=[vmem] * len(outs) if many else vmem,
        scratch_shapes=list(scratch),
        compiler_params=pltpu.CompilerParams(vmem_limit_bytes=grant * 2**20),
    )(*args)


def shape(dims, dtype):
    return jax.ShapeDtypeStruct(dims, dtype)


def exchange(value, axes):
    return lax.all_to_all(value, axes, 0, 0, tiled=True)


def shards(orbitals, inverse_intersection, half_rotated, chol_full, fields):
    orb = orbitals[0]
    packed = call(
        pack_kernel, shape((32, 976), bf16), orb, chol_full[0],
        scratch=[pltpu.VMEM((64, 200), f32), pltpu.VMEM((32, 1024), bf16), pltpu.SemaphoreType.DMA((2,))],
        hbm=(0, 1), grant=60,
    )
    ring = lax.all_gather(packed, RING, axis=0, tiled=True)
    own, send = call(select_kernel, [shape((8, 32, 1152), bf16)] * 2, ring.reshape(2, 8, 32, 976))
    swap_core = [(0, 1), (1, 0)]
    got = lax.ppermute(send, "core", swap_core)
    first, partial = call(
        bias_kernel, [shape((1024, 256), bf16), shape((16, 1, 128), f32)],
        fields, own, got, inverse_intersection[0], half_rotated[0],
        scratch=[pltpu.VMEM((256, 256), bf16), pltpu.VMEM((256, 256), bf16)], smem=1,
    )
    along_z = exchange(partial, CHOL)
    summed = call(sum_kernel, shape((16, 1, 128), f32), along_z)
    everywhere = exchange(summed, PLANE)
    pieces = call(operator_kernel, shape((16, 32, 640), bf16), everywhere, own, got)
    mine = exchange(pieces, PLANE)
    other = lax.ppermute(mine, "core", swap_core)
    out = call(
        taylor_kernel, shape((64, 200), f32), orb, mine, other, first,
        scratch=[pltpu.VMEM((1024, 1024), bf16), pltpu.VMEM((1024, 128), f32)],
    )
    return out[None]


def solution(mesh):
    fine = Mesh(mesh.devices.reshape(8, 2, 4, 4, 2), ("zl", "core", "y", "x", "zh"))
    return jax.shard_map(
        shards,
        mesh=fine,
        in_specs=(
            P(WALK, CHOL, None),
            P(WALK, None, None),
            P(CHOL, None, None),
            P(CHOL, WALK, None),
            P(CHOL, WALK),
        ),
        out_specs=P(WALK, CHOL, None),
        check_vma=False,
    )
```

```python
import jax
import jax.numpy as jnp
from jax import lax
from jax.experimental import pallas as pl
from jax.experimental.pallas import tpu as pltpu
from jax.sharding import Mesh, PartitionSpec as P

TAYLOR = 5
field_scale = 0.4
f32, bf16 = jnp.float32, jnp.bfloat16

CHOL = ("zl", "core")
WALK = ("y", "x", "zh")
PLANE = ("y", "x")
RING = ("zh", "zl")


def iota(shape, dim):
    return lax.broadcasted_iota(jnp.int32, shape, dim)


def plane_index():
    return lax.axis_index("y") * 4 + lax.axis_index("x")


def chol_index():
    return lax.axis_index("zl") * 2 + lax.axis_index("core")


def pack_kernel(orb_hbm, chol_hbm, out_ref, orb_ref, chol_ref, sems):
    copies = [pltpu.make_async_copy(chol_hbm, chol_ref, sems.at[0]), pltpu.make_async_copy(orb_hbm, orb_ref, sems.at[1])]
    for copy in copies:
        copy.start()
    p = plane_index()
    start = p // 2

    def block(d):
        col = pl.multiple_of(lax.rem(start + d, 8) * 128, 128)
        return chol_ref[:, pl.ds(col, 128)]

    copies[0].wait()
    for d in range(4):
        out_ref[:, 128 * d:128 * d + 128] = block(d)
    last = block(4).astype(f32)
    half = jnp.bitwise_xor(jnp.bitwise_and(p, 1), (start >= 4).astype(jnp.int32))
    last = jnp.where(half == 1, pltpu.roll(last, 64, 1), last)
    copies[1].wait()
    low = jnp.concatenate([orb_ref[...], jnp.zeros((64, 56), f32)], axis=1)
    top, bottom = low[0:32], low[32:64]
    lane = iota((32, 128), 1)
    out_ref[:, 512:640] = jnp.where(lane < 64, last, pltpu.roll(bottom[:, 128:256], 64, 1)).astype(bf16)
    out_ref[:, 640:768] = top[:, 0:128].astype(bf16)
    out_ref[:, 768:896] = bottom[:, 0:128].astype(bf16)
    ends = jnp.where(lane < 72, top[:, 128:256], pltpu.roll(bottom[:, 128:256], 8, 1))
    out_ref[:, 896:976] = ends[:, 0:80].astype(bf16)


def select_kernel(ring_ref, own_ref, send_ref):
    k, h = lax.axis_index("core"), lax.axis_index("zh")
    lane = iota((32, 128), 1)
    for j in range(8):
        for half, target in ((k, own_ref), (1 - k, send_ref)):
            target[j, :, 0:512] = ring_ref[half, j, :, 0:512]
            tail = ring_ref[half, j, :, 512:640].astype(f32)
            target[j, :, 512:640] = jnp.where(lane < 64, tail, 0.0).astype(bf16)
        middle = ring_ref[h, j, :, 512:640].astype(f32)
        ends = jnp.concatenate([ring_ref[h, j, :, 896:976].astype(f32), jnp.zeros((32, 48), f32)], axis=1)
        top = jnp.where(lane < 72, ends, 0.0).astype(bf16)
        bottom = jnp.where(lane < 64, pltpu.roll(middle, 64, 1), jnp.where(lane < 72, pltpu.roll(ends, 120, 1), 0.0))
        bottom = bottom.astype(bf16)
        for target in (own_ref, send_ref):
            target[j, :, 640:768] = ring_ref[h, j, :, 640:768]
            target[j, :, 768:896] = top
            target[j, :, 896:1024] = ring_ref[h, j, :, 768:896]
            target[j, :, 1024:1152] = bottom


def bias_kernel(field_ref, own_ref, got_ref, inv_ref, hr_ref, term_ref, out_ref, inv_low, inv_high):
    k = lax.axis_index("core")
    for j in range(8):
        for source, core in ((own_ref, k), (got_ref, 1 - k)):
            row = pl.multiple_of((2 * j + core) * 64, 64)
            term_ref[pl.ds(row, 32), :] = source[j, :, 640:896]
            term_ref[pl.ds(row + 32, 32), :] = source[j, :, 896:1152]
    inverse = inv_ref[...]
    wide = jnp.concatenate([inverse, jnp.zeros((200, 56), f32)], axis=1)
    full = jnp.concatenate([wide, jnp.zeros((56, 256), f32)], axis=0)
    high = full.astype(bf16)
    inv_high[...] = high
    inv_low[...] = (full - high.astype(f32)).astype(bf16)
    term = term_ref[...]
    theta = jnp.dot(term, inv_high[...], preferred_element_type=f32)
    theta += jnp.dot(term, inv_low[...], preferred_element_type=f32)
    theta_high = theta.astype(bf16)
    theta_low = (theta - theta_high.astype(f32)).astype(bf16)
    rotated = hr_ref[...]
    product = jnp.dot(rotated, theta_high, preferred_element_type=f32)
    product += jnp.dot(rotated, theta_low, preferred_element_type=f32)
    diagonal = jnp.where(iota((200, 256), 0) == iota((200, 256), 1), product, 0.0)
    raw_bias = jnp.sum(jnp.sum(diagonal, axis=0, keepdims=True), axis=1, keepdims=True)
    shifted = field_scale * (field_ref[0, 0] - jnp.clip(raw_bias, -1.0, 1.0))
    row = jnp.where(iota((1, 128), 1) == chol_index(), shifted, 0.0)
    for j in range(16):
        out_ref[j] = row


def sum_kernel(in_ref, out_ref):
    row = jnp.sum(in_ref[...], axis=0)
    for j in range(16):
        out_ref[j] = row


def operator_kernel(in_ref, own_ref, got_ref, out_ref):
    k = lax.axis_index("core")
    by_walker = jnp.concatenate([in_ref[:, 0, :], jnp.zeros((112, 128), f32)], axis=0)
    high = by_walker.astype(bf16)
    rest = (by_walker - high.astype(f32)).astype(bf16)
    g, q = iota((128, 256), 0), iota((128, 256), 1) >> 4
    vector = 2 * (q & 7) + jnp.where(q < 8, k, 1 - k)
    pick = jnp.where(g == vector, 1.0, 0.0).astype(bf16)
    walkers = jnp.where((iota((256, 128), 0) >> 4) == iota((256, 128), 1), 1.0, 0.0).astype(bf16)
    same = (iota((256, 256), 0) & 15) == (iota((256, 256), 1) & 15)

    def weights(part):
        spread = jnp.dot(part, pick, preferred_element_type=f32).astype(bf16)
        full = jnp.dot(walkers, spread, preferred_element_type=f32)
        return jnp.where(same, full, 0.0).astype(bf16)

    w_high, w_rest = weights(high), weights(rest)
    for i in range(2):
        rows = slice(16 * i, 16 * i + 16)
        own = own_ref[:, rows, 0:640].reshape(128, 640)
        got = got_ref[:, rows, 0:640].reshape(128, 640)
        vectors = jnp.concatenate([own, got], axis=0)
        value = jnp.dot(w_rest, vectors, preferred_element_type=f32)
        value += jnp.dot(w_high, vectors, preferred_element_type=f32)
        out_ref[:, rows, :] = value.astype(bf16).reshape(16, 16, 640)


def place_rows(source, core, op, tail):
    for p in range(16):
        row = pl.multiple_of(64 * p + 32 * core, 32)
        for d in range(4):
            col = ((p // 2 + d) % 8) * 128
            op[pl.ds(row, 32), col:col + 128] = source[p, :, 128 * d:128 * d + 128]
        tail[pl.ds(row, 32), :] = source[p, :, 512:640].astype(f32)


def place_kernel(mine_ref, op, tail):
    place_rows(mine_ref, lax.axis_index("core"), op, tail)


def taylor_kernel(orb_ref, other_ref, first_ref, op_in, tail_in, out_ref, op, tail):
    del op_in, tail_in
    place_rows(other_ref, 1 - lax.axis_index("core"), op, tail)
    for i in range(8):
        for d in range(1, 4):
            j = (i + d) % 8
            block = op[128 * i:128 * i + 128, 128 * j:128 * j + 128].astype(f32)
            op[128 * j:128 * j + 128, 128 * i:128 * i + 128] = block.T.astype(bf16)
    left = iota((64, 128), 1) < 64
    for i in range(4):
        j = i + 4
        near = tail[128 * i:128 * i + 128, :]
        far = tail[128 * j:128 * j + 128, :].T[0:64]
        top = jnp.where(left, near[0:64], far)
        bottom = jnp.where(left, far, pltpu.roll(near[64:128], 64, 1))
        block = jnp.concatenate([top, bottom], axis=0)
        op[128 * i:128 * i + 128, 128 * j:128 * j + 128] = block.astype(bf16)
        op[128 * j:128 * j + 128, 128 * i:128 * i + 128] = block.T.astype(bf16)
    own = pl.multiple_of(chol_index() * 64, 64)
    own_rows = op[pl.ds(own, 64), :]
    power, share = own_rows, 1.0
    series = power.astype(f32)
    for degree in range(2, TAYLOR + 1):
        product = jnp.dot(power, op[...], preferred_element_type=f32)
        share = share / degree
        series += product * share
        power = product.astype(bf16)
    high = series.astype(bf16)
    rest = (series - high.astype(f32)).astype(bf16)
    first = first_ref[...]
    total = jnp.dot(rest, first, preferred_element_type=f32)
    total += jnp.dot(high, first, preferred_element_type=f32)
    out_ref[...] = orb_ref[...] + total[:, :200]


def call(body, outs, *args, scratch=(), smem=0, hbm=(), grant=40, aliases=None):
    vmem = pl.BlockSpec(memory_space=pltpu.VMEM)
    specs = [pl.BlockSpec(memory_space=pltpu.SMEM)] * smem + [vmem] * (len(args) - smem)
    for i in hbm:
        specs[i] = pl.BlockSpec(memory_space=pl.ANY)
    many = isinstance(outs, (list, tuple))
    return pl.pallas_call(
        body,
        out_shape=outs,
        in_specs=specs,
        out_specs=[vmem] * len(outs) if many else vmem,
        scratch_shapes=list(scratch),
        input_output_aliases=aliases or {},
        compiler_params=pltpu.CompilerParams(vmem_limit_bytes=grant * 2**20),
    )(*args)


def shape(dims, dtype):
    return jax.ShapeDtypeStruct(dims, dtype)


def exchange(value, axes):
    return lax.all_to_all(value, axes, 0, 0, tiled=True)


def shards(orbitals, inverse_intersection, half_rotated, chol_full, fields):
    orb = orbitals[0]
    packed = call(
        pack_kernel, shape((32, 976), bf16), orb, chol_full[0],
        scratch=[pltpu.VMEM((64, 200), f32), pltpu.VMEM((32, 1024), bf16), pltpu.SemaphoreType.DMA((2,))],
        hbm=(0, 1), grant=60,
    )
    ring = lax.all_gather(packed, RING, axis=0, tiled=True)
    own, send = call(select_kernel, [shape((8, 32, 1152), bf16)] * 2, ring.reshape(2, 8, 32, 976))
    swap_core = [(0, 1), (1, 0)]
    got = lax.ppermute(send, "core", swap_core)
    first, partial = call(
        bias_kernel, [shape((1024, 256), bf16), shape((16, 1, 128), f32)],
        fields, own, got, inverse_intersection[0], half_rotated[0],
        scratch=[pltpu.VMEM((256, 256), bf16), pltpu.VMEM((256, 256), bf16)], smem=1,
    )
    along_z = exchange(partial, CHOL)
    summed = call(sum_kernel, shape((16, 1, 128), f32), along_z)
    everywhere = exchange(summed, PLANE)
    pieces = call(operator_kernel, shape((16, 32, 640), bf16), everywhere, own, got)
    mine = exchange(pieces, PLANE)
    other = lax.ppermute(mine, "core", swap_core)
    halves = [shape((1024, 1024), bf16), shape((1024, 128), f32)]
    op, tail = call(place_kernel, halves, mine)
    out, _, _ = call(
        taylor_kernel, [shape((64, 200), f32)] + halves, orb, other, first, op, tail, aliases={3: 1, 4: 2},
    )
    return out[None]


def solution(mesh):
    fine = Mesh(mesh.devices.reshape(8, 2, 4, 4, 2), ("zl", "core", "y", "x", "zh"))
    return jax.shard_map(
        shards,
        mesh=fine,
        in_specs=(
            P(WALK, CHOL, None),
            P(WALK, None, None),
            P(CHOL, None, None),
            P(CHOL, WALK, None),
            P(CHOL, WALK),
        ),
        out_specs=P(WALK, CHOL, None),
        check_vma=False,
    )
```

```python
import jax
import jax.numpy as jnp
from jax import lax
from jax.experimental import pallas as pl
from jax.experimental.pallas import tpu as pltpu
from jax.sharding import Mesh, PartitionSpec as P

TAYLOR = 5
field_scale = 0.4
f32, bf16 = jnp.float32, jnp.bfloat16

CHOL = ("zl", "core")
WALK = ("y", "x", "zh")
PLANE = ("y", "x")
RING = ("zh", "zl")


def iota(shape, dim):
    return lax.broadcasted_iota(jnp.int32, shape, dim)


def plane_index():
    return lax.axis_index("y") * 4 + lax.axis_index("x")


def chol_index():
    return lax.axis_index("zl") * 2 + lax.axis_index("core")


def pack_kernel(orb_hbm, chol_hbm, out_ref, orb_ref, chol_ref, sems):
    copies = [pltpu.make_async_copy(chol_hbm, chol_ref, sems.at[0]), pltpu.make_async_copy(orb_hbm, orb_ref, sems.at[1])]
    for copy in copies:
        copy.start()
    p = plane_index()
    start = p // 2

    def block(d):
        col = pl.multiple_of(lax.rem(start + d, 8) * 128, 128)
        return chol_ref[:, pl.ds(col, 128)]

    copies[0].wait()
    for d in range(4):
        out_ref[:, 128 * d:128 * d + 128] = block(d)
    last = block(4).astype(f32)
    half = jnp.bitwise_xor(jnp.bitwise_and(p, 1), (start >= 4).astype(jnp.int32))
    last = jnp.where(half == 1, pltpu.roll(last, 64, 1), last)
    copies[1].wait()
    low = jnp.concatenate([orb_ref[...], jnp.zeros((64, 56), f32)], axis=1)
    top, bottom = low[0:32], low[32:64]
    lane = iota((32, 128), 1)
    out_ref[:, 512:640] = jnp.where(lane < 64, last, pltpu.roll(bottom[:, 128:256], 64, 1)).astype(bf16)
    out_ref[:, 640:768] = top[:, 0:128].astype(bf16)
    out_ref[:, 768:896] = bottom[:, 0:128].astype(bf16)
    ends = jnp.where(lane < 72, top[:, 128:256], pltpu.roll(bottom[:, 128:256], 8, 1))
    out_ref[:, 896:976] = ends[:, 0:80].astype(bf16)


def select_kernel(ring_ref, own_ref, send_ref):
    k, h = lax.axis_index("core"), lax.axis_index("zh")
    lane = iota((32, 128), 1)
    for j in range(8):
        for half, target in ((k, own_ref), (1 - k, send_ref)):
            target[j, :, 0:512] = ring_ref[half, j, :, 0:512]
            tail = ring_ref[half, j, :, 512:640].astype(f32)
            target[j, :, 512:640] = jnp.where(lane < 64, tail, 0.0).astype(bf16)
        middle = ring_ref[h, j, :, 512:640].astype(f32)
        ends = jnp.concatenate([ring_ref[h, j, :, 896:976].astype(f32), jnp.zeros((32, 48), f32)], axis=1)
        top = jnp.where(lane < 72, ends, 0.0).astype(bf16)
        bottom = jnp.where(lane < 64, pltpu.roll(middle, 64, 1), jnp.where(lane < 72, pltpu.roll(ends, 120, 1), 0.0))
        bottom = bottom.astype(bf16)
        for target in (own_ref, send_ref):
            target[j, :, 640:768] = ring_ref[h, j, :, 640:768]
            target[j, :, 768:896] = top
            target[j, :, 896:1024] = ring_ref[h, j, :, 768:896]
            target[j, :, 1024:1152] = bottom


def bias_kernel(field_ref, own_ref, got_ref, inv_ref, hr_ref, term_ref, out_ref, inv_low, inv_high):
    k = lax.axis_index("core")
    for j in range(8):
        for source, core in ((own_ref, k), (got_ref, 1 - k)):
            row = pl.multiple_of((2 * j + core) * 64, 64)
            term_ref[pl.ds(row, 32), :] = source[j, :, 640:896]
            term_ref[pl.ds(row + 32, 32), :] = source[j, :, 896:1152]
    inverse = inv_ref[...]
    wide = jnp.concatenate([inverse, jnp.zeros((200, 56), f32)], axis=1)
    full = jnp.concatenate([wide, jnp.zeros((56, 256), f32)], axis=0)
    high = full.astype(bf16)
    inv_high[...] = high
    inv_low[...] = (full - high.astype(f32)).astype(bf16)
    term = term_ref[...]
    theta = jnp.dot(term, inv_high[...], preferred_element_type=f32)
    theta += jnp.dot(term, inv_low[...], preferred_element_type=f32)
    theta_high = theta.astype(bf16)
    theta_low = (theta - theta_high.astype(f32)).astype(bf16)
    rotated = hr_ref[...]
    product = jnp.dot(rotated, theta_high, preferred_element_type=f32)
    product += jnp.dot(rotated, theta_low, preferred_element_type=f32)
    diagonal = jnp.where(iota((200, 256), 0) == iota((200, 256), 1), product, 0.0)
    raw_bias = jnp.sum(jnp.sum(diagonal, axis=0, keepdims=True), axis=1, keepdims=True)
    shifted = field_scale * (field_ref[0, 0] - jnp.clip(raw_bias, -1.0, 1.0))
    row = jnp.where(iota((1, 128), 1) == chol_index(), shifted, 0.0)
    for j in range(16):
        out_ref[j] = row


def sum_kernel(in_ref, out_ref):
    row = jnp.sum(in_ref[...], axis=0)
    for j in range(16):
        out_ref[j] = row


def operator_kernel(in_ref, own_ref, got_ref, out_ref):
    k = lax.axis_index("core")
    by_walker = jnp.concatenate([in_ref[:, 0, :], jnp.zeros((112, 128), f32)], axis=0)
    high = by_walker.astype(bf16)
    rest = (by_walker - high.astype(f32)).astype(bf16)
    g, q = iota((128, 256), 0), iota((128, 256), 1) >> 4
    vector = 2 * (q & 7) + jnp.where(q < 8, k, 1 - k)
    pick = jnp.where(g == vector, 1.0, 0.0).astype(bf16)
    walkers = jnp.where((iota((256, 128), 0) >> 4) == iota((256, 128), 1), 1.0, 0.0).astype(bf16)
    same = (iota((256, 256), 0) & 15) == (iota((256, 256), 1) & 15)

    def weights(part):
        spread = jnp.dot(part, pick, preferred_element_type=f32).astype(bf16)
        full = jnp.dot(walkers, spread, preferred_element_type=f32)
        return jnp.where(same, full, 0.0).astype(bf16)

    w_high, w_rest = weights(high), weights(rest)
    for i in range(2):
        rows = slice(16 * i, 16 * i + 16)
        own = own_ref[:, rows, 0:640].reshape(128, 640)
        got = got_ref[:, rows, 0:640].reshape(128, 640)
        vectors = jnp.concatenate([own, got], axis=0)
        value = jnp.dot(w_rest, vectors, preferred_element_type=f32)
        value += jnp.dot(w_high, vectors, preferred_element_type=f32)
        out_ref[:, rows, :] = value.astype(bf16).reshape(16, 16, 640)


def place_rows(source, core, op, tail):
    for p in range(16):
        row = pl.multiple_of(64 * p + 32 * core, 32)
        for d in range(4):
            col = ((p // 2 + d) % 8) * 128
            op[pl.ds(row, 32), col:col + 128] = source[p, :, 128 * d:128 * d + 128]
        tail[pl.ds(row, 32), :] = source[p, :, 512:640].astype(f32)


def place_kernel(mine_ref, op, tail):
    place_rows(mine_ref, lax.axis_index("core"), op, tail)


def taylor_kernel(orb_ref, other_ref, first_ref, op_in, tail_in, out_ref, op, tail):
    del op_in, tail_in
    place_rows(other_ref, 1 - lax.axis_index("core"), op, tail)
    for i in range(8):
        for d in range(1, 4):
            j = (i + d) % 8
            op[128 * j:128 * j + 128, 128 * i:128 * i + 128] = op[128 * i:128 * i + 128, 128 * j:128 * j + 128].T
    left = iota((64, 128), 1) < 64
    for i in range(4):
        j = i + 4
        near = tail[128 * i:128 * i + 128, :]
        far = tail[128 * j:128 * j + 128, :].T[0:64]
        top = jnp.where(left, near[0:64], far)
        bottom = jnp.where(left, far, pltpu.roll(near[64:128], 64, 1))
        block = jnp.concatenate([top, bottom], axis=0)
        op[128 * i:128 * i + 128, 128 * j:128 * j + 128] = block.astype(bf16)
        op[128 * j:128 * j + 128, 128 * i:128 * i + 128] = block.T.astype(bf16)
    own = pl.multiple_of(chol_index() * 64, 64)
    own_rows = op[pl.ds(own, 64), :]
    power, share = own_rows, 1.0
    series = power.astype(f32)
    for degree in range(2, TAYLOR + 1):
        product = jnp.dot(power, op[...], preferred_element_type=f32)
        share = share / degree
        series += product * share
        power = product.astype(bf16)
    high = series.astype(bf16)
    rest = (series - high.astype(f32)).astype(bf16)
    first = first_ref[...]
    total = jnp.dot(rest, first, preferred_element_type=f32)
    total += jnp.dot(high, first, preferred_element_type=f32)
    out_ref[...] = orb_ref[...] + total[:, :200]


def call(body, outs, *args, scratch=(), smem=0, hbm=(), grant=40, aliases=None):
    vmem = pl.BlockSpec(memory_space=pltpu.VMEM)
    specs = [pl.BlockSpec(memory_space=pltpu.SMEM)] * smem + [vmem] * (len(args) - smem)
    for i in hbm:
        specs[i] = pl.BlockSpec(memory_space=pl.ANY)
    many = isinstance(outs, (list, tuple))
    return pl.pallas_call(
        body,
        out_shape=outs,
        in_specs=specs,
        out_specs=[vmem] * len(outs) if many else vmem,
        scratch_shapes=list(scratch),
        input_output_aliases=aliases or {},
        compiler_params=pltpu.CompilerParams(vmem_limit_bytes=grant * 2**20),
    )(*args)


def shape(dims, dtype):
    return jax.ShapeDtypeStruct(dims, dtype)


def exchange(value, axes):
    return lax.all_to_all(value, axes, 0, 0, tiled=True)


def shards(orbitals, inverse_intersection, half_rotated, chol_full, fields):
    orb = orbitals[0]
    packed = call(
        pack_kernel, shape((32, 976), bf16), orb, chol_full[0],
        scratch=[pltpu.VMEM((64, 200), f32), pltpu.VMEM((32, 1024), bf16), pltpu.SemaphoreType.DMA((2,))],
        hbm=(0, 1), grant=60,
    )
    ring = lax.all_gather(packed, RING, axis=0, tiled=True)
    own, send = call(select_kernel, [shape((8, 32, 1152), bf16)] * 2, ring.reshape(2, 8, 32, 976))
    swap_core = [(0, 1), (1, 0)]
    got = lax.ppermute(send, "core", swap_core)
    first, partial = call(
        bias_kernel, [shape((1024, 256), bf16), shape((16, 1, 128), f32)],
        fields, own, got, inverse_intersection[0], half_rotated[0],
        scratch=[pltpu.VMEM((256, 256), bf16), pltpu.VMEM((256, 256), bf16)], smem=1,
    )
    along_z = exchange(partial, CHOL)
    summed = call(sum_kernel, shape((16, 1, 128), f32), along_z)
    everywhere = exchange(summed, PLANE)
    pieces = call(operator_kernel, shape((16, 32, 640), bf16), everywhere, own, got)
    mine = exchange(pieces, PLANE)
    other = lax.ppermute(mine, "core", swap_core)
    halves = [shape((1024, 1024), bf16), shape((1024, 128), f32)]
    op, tail = call(place_kernel, halves, mine)
    out, _, _ = call(
        taylor_kernel, [shape((64, 200), f32)] + halves, orb, other, first, op, tail, aliases={3: 1, 4: 2},
    )
    return out[None]


def solution(mesh):
    fine = Mesh(mesh.devices.reshape(8, 2, 4, 4, 2), ("zl", "core", "y", "x", "zh"))
    return jax.shard_map(
        shards,
        mesh=fine,
        in_specs=(
            P(WALK, CHOL, None),
            P(WALK, None, None),
            P(CHOL, None, None),
            P(CHOL, WALK, None),
            P(CHOL, WALK),
        ),
        out_specs=P(WALK, CHOL, None),
        check_vma=False,
    )
```
